32 devices in a mesh: dp: 8 (over y, x, core), expert: 4 (over z).
Axes of the slice: x: 2, y: 2, z: 4, core: 2. Of those that a mesh axis runs over, the one named last changes fastest.
Arguments:
- attended: bfloat16 [2560, 1536], P(('dp', 'expert')), may hold values from -6 to 6
- residual: bfloat16 [2560, 1536], P(('dp', 'expert')), may hold values from -16 to 16
- out_weight: bfloat16 [1536, 1536], replicated, may hold values from -0.15625 to 0.15625
- norm_gain: float32 [1536], replicated, may hold values from 0.1 to 1.9
- final_gain: float32 [1536], replicated, may hold values from 0.5 to 1.5
- routes: int32 [2560, 8], P(('dp', 'expert')), may hold values from 0 to 19, as said below
- gate_logits: int32 [2560, 8], P(('dp', 'expert')), may hold values from -1 to 1
- placement: int32 [20], replicated, may hold values from 0 to 19, each once
- gate_up: bfloat16 [20, 1536, 1024], P('expert', 'dp'), may hold values from -0.15625 to 0.15625
- down_weight: bfloat16 [20, 1536, 512], P('expert', 'dp'), may hold values from -0.5 to 0.5
Outputs:
- stream: bfloat16 [2560, 1536], P(('dp', 'expert'))
- normed: bfloat16 [2560, 1536], P(('dp', 'expert'))
The draws below stay inside these ranges and needn't reach their ends.
Inputs may be any that keep to these rules, and one draw needn't show every extreme that they name: `routes`: each row names 8 different experts. Within the rows of one device no expert is named by more than 64 rows, and some expert is named by exactly 64 rows on every device. `placement`: slot s lies on index s // 5 of the expert axis; every expert is held by exactly one slot.
All inputs are finite; a program needn't handle non-finite values.
Results may differ from the reference program's by a relative error of at most 0.006.
Values may be sent and summed in bfloat16 or wider, within the bound.
No kernel may reach another device: no remote copies, remote signals or barrier semaphores. Data moves between devices by JAX's collectives and lax.ppermute only.
A program may use at most 128 MiB of HBM per device.

```python
import math
import jax
import jax.numpy as jnp
from jax import lax

D = 1536
F = 512
TOP = 8
TOK_DEV = 80
EXPERTS = 20
TOKENS = 2560
CAP = 64


def draw_residual(key, part):
    first, second, third = jax.random.split(key, 3)
    row_scale = jnp.exp(jax.random.uniform(first, (TOKENS, 1), jnp.float32, math.log(0.3), math.log(3.0)))
    col_scale = jnp.exp(jax.random.uniform(second, (1, D), jnp.float32, math.log(0.3), math.log(3.0)))
    base = jax.random.normal(third, (TOKENS, D), jnp.float32)
    return jnp.clip(base * row_scale * col_scale, -16.0, 16.0).astype(jnp.bfloat16)


def random_ranks(key, blocks, length):
    scores = jax.random.randint(key, (blocks, length), 0, 1 << 20) * length + jnp.arange(length, dtype=jnp.int32)
    order = jnp.argsort(scores, axis=1, stable=True)
    return jnp.argsort(order, axis=1, stable=True).astype(jnp.int32)


def draw_routes(key, part):
    blocks = TOKENS // TOK_DEV
    key_perm, key_sub, key_first, key_second, key_size, key_roll = jax.random.split(key, 6)
    order = jax.random.permutation(key_perm, EXPERTS).astype(jnp.int32)
    hot_first = order[0]
    hot_second = order[1]
    others = order[2:]
    sub_scores = jax.random.randint(key_sub, (blocks, EXPERTS - 2), 0, 1 << 20) * (EXPERTS - 2) + jnp.arange(EXPERTS - 2, dtype=jnp.int32)
    sub_order = jnp.argsort(sub_scores, axis=1, stable=True).astype(jnp.int32)
    others_block = others[sub_order]
    in_first = random_ranks(key_first, blocks, TOK_DEV) < CAP
    in_second = random_ranks(key_second, blocks, TOK_DEV) < CAP
    hot_count = in_first.astype(jnp.int32) + in_second.astype(jnp.int32)
    needed = TOP - hot_count
    offset = jnp.cumsum(needed, axis=1) - needed
    lowest = max(-(-(TOK_DEV * TOP - 2 * CAP) // CAP), TOP)
    cycle = jax.random.randint(key_size, (blocks, 1, 1), lowest, EXPERTS - 1)
    column = jnp.arange(TOP, dtype=jnp.int32)[None, None, :]
    place = (offset[..., None] + column - hot_count[..., None]) % cycle
    spread = jnp.broadcast_to(others_block[:, None, :], (blocks, TOK_DEV, EXPERTS - 2))
    other_pick = jnp.take_along_axis(spread, place, axis=2)
    hot_pick = jnp.where((column == 0) & in_first[..., None], hot_first, hot_second)
    chosen = jnp.where(column < hot_count[..., None], hot_pick, other_pick)
    shift = jax.random.randint(key_roll, (blocks, TOK_DEV, 1), 0, TOP)
    rolled = jnp.take_along_axis(chosen, (column + shift) % TOP, axis=2)
    return rolled.reshape(TOKENS, TOP).astype(jnp.int32)


def with_ends(drawn, key, least, high):
    longest = drawn.shape.index(max(drawn.shape))
    spots = []
    for shift in (0, 1):
        where = [jax.random.randint(jax.random.fold_in(key, axis), (), 0, length) for axis, length in enumerate(drawn.shape)]
        where[longest] = (where[longest] + shift) % drawn.shape[longest]
        spots.append(tuple(where))
    return drawn.at[spots[0]].set(least).at[spots[1]].set(high)


def block_levels(own_key, shape, shards, low, high):
    factor_of = 1.0
    for dim, blocks in shards:
        heights = jax.random.uniform(jax.random.fold_in(jax.random.fold_in(own_key, 6), dim), (blocks,), jnp.float32, low / len(shards), high / len(shards))
        factor_of = factor_of * jnp.repeat(jnp.exp(heights), shape[dim] // blocks).reshape((-1,) + (1,) * (len(shape) - 1 - dim))
    return factor_of


def gaussian(stream_key, shape, scale, reach, cuts=(), kind=jnp.bfloat16):
    values = jax.random.normal(stream_key, shape, jnp.float32) * scale
    if len(cuts) > 0:
        values = block_levels(stream_key, shape, cuts, -0.22, 0.18) * values
    return jnp.clip(values, min=-reach, max=reach).astype(kind)


def setup_inputs(seed: int = 0) -> dict:
    streams_of = jax.random.split(jax.random.key(seed), 11)
    attended = gaussian(streams_of[0], (TOKENS, D), 1.0, 6.0, ((0, 32),))
    residual = draw_residual(jax.random.fold_in(streams_of[10], 71), 0)
    out_weight = gaussian(streams_of[2], (D, D), D ** -0.5, 0.15625)
    norm_gain = jnp.clip(1.0 + 0.18 * jax.random.normal(streams_of[3], (D,), jnp.float32), 0.1, 1.9)
    final_gain = jnp.clip(1.0 + 0.1 * jax.random.normal(streams_of[4], (D,), jnp.float32), 0.5, 1.5)
    routes = draw_routes(jax.random.fold_in(streams_of[10], 71), 0)
    gate_logits = with_ends(jax.random.randint(streams_of[6], (TOKENS, TOP), -1, 2), jax.random.fold_in(streams_of[6], 1), -1, 1).astype(jnp.int32)
    placement = jax.random.permutation(streams_of[7], EXPERTS).astype(jnp.int32)
    gate_up = gaussian(streams_of[8], (EXPERTS, D, 2 * F), D ** -0.5, 0.15625, ((0, 4), (1, 8)))
    down_weight = gaussian(streams_of[9], (EXPERTS, D, F), (F // 4) ** -0.5, 0.5, ((0, 4), (1, 8)))
    return {"attended": attended, "residual": residual, "out_weight": out_weight, "norm_gain": norm_gain, "final_gain": final_gain, "routes": routes, "gate_logits": gate_logits, "placement": placement, "gate_up": gate_up, "down_weight": down_weight}


EPS = 1e-06
LOGIT_SCALE = 0.5

def normalize(values, gain):
    return values * lax.rsqrt(lax.optimization_barrier(jnp.mean(values * values, axis=-1, keepdims=True)) + EPS) * gain

def reference(attended, residual, out_weight, norm_gain, final_gain, routes, gate_logits, placement, gate_up, down_weight):
    mixed = residual.astype(jnp.float32) + jnp.dot(attended, out_weight, preferred_element_type=jnp.float32)
    stored = lax.optimization_barrier(mixed.astype(jnp.bfloat16))
    stream_in = stored.astype(jnp.float32)
    normed_in = normalize(stream_in, norm_gain).astype(jnp.bfloat16)
    scores = jnp.exp(gate_logits.astype(jnp.float32) * LOGIT_SCALE)
    gate = scores / lax.optimization_barrier(jnp.sum(scores, axis=-1, keepdims=True))
    slot_of = jnp.zeros((EXPERTS,), jnp.int32).at[placement].set(jnp.arange(EXPERTS, dtype=jnp.int32))
    route_slot = slot_of[routes].reshape(-1)
    gate_flat = gate.reshape(-1)
    assigned = TOKENS * TOP
    row_of = jnp.arange(assigned, dtype=jnp.int32) // TOP
    limit = TOKENS // TOK_DEV * CAP

    def one_slot(slot, total):
        found = jnp.nonzero(route_slot == slot, size=limit, fill_value=assigned)[0].astype(jnp.int32)
        valid = found < assigned
        clamped = jnp.minimum(found, assigned - 1)
        token_rows = row_of[clamped]
        chosen = normed_in[token_rows]
        gate_vals = jnp.dot(chosen, gate_up[slot], preferred_element_type=jnp.float32)
        hidden = (jax.nn.silu(gate_vals[:, :F]) * gate_vals[:, F:]).astype(jnp.bfloat16)
        produced = jnp.dot(hidden, down_weight[slot].T, preferred_element_type=jnp.float32).astype(jnp.bfloat16)
        weight = jnp.where(valid, gate_flat[clamped], jnp.zeros((), jnp.float32))
        return total.at[token_rows].add(weight[:, None] * produced.astype(jnp.float32))
    branch = lax.fori_loop(0, EXPERTS, one_slot, jnp.zeros((TOKENS, D), jnp.float32))
    total = stream_in + branch
    return (total.astype(jnp.bfloat16), normalize(total, final_gain).astype(jnp.bfloat16))
```

```python
import functools

import jax
import jax.numpy as jnp
from jax import lax
from jax.experimental import pallas as pl
from jax.experimental.pallas import tpu as pltpu
from jax.sharding import PartitionSpec as P

EPS = 1e-06
LOGIT_SCALE = 0.5
LANES = 128
LOW = 64
QUAD = 4


def normalize(values, gain):
    return values * lax.rsqrt(jnp.mean(values * values, axis=-1, keepdims=True) + EPS) * gain


def combine_weights(logits):
    scores = jnp.exp(logits.astype(jnp.float32) * LOGIT_SCALE)
    return scores / jnp.sum(scores, axis=-1, keepdims=True)


def slot_gates(routes, logits, placement):
    gates = combine_weights(logits)
    hit = routes[:, :, None] == placement[None, None, :]
    return jnp.sum(jnp.where(hit, gates[:, :, None], 0.0), axis=1)


def gate_lanes(gates):
    high = gates.astype(jnp.bfloat16)
    low = (gates - high.astype(jnp.float32)).astype(jnp.bfloat16)
    pad = ((0, 0), (0, LOW - gates.shape[1]))
    return jnp.concatenate([jnp.pad(high, pad), jnp.pad(low, pad)], axis=1)


def swap_blocks(values, index, blocks):
    lead = values.shape[:-1]
    out = values.reshape(*lead, blocks, -1)
    bit = 1
    while bit < blocks:
        order = [m ^ bit for m in range(blocks)]
        swapped = jnp.concatenate([out[..., m : m + 1, :] for m in order], axis=-2)
        out = jnp.where((index & bit) != 0, swapped, out)
        bit *= 2
    return out.reshape(values.shape)


def up_kernel(rows, place_ref, x_ref, *refs):
    own, nbr, out_ref = refs[:rows], refs[rows : 2 * rows], refs[2 * rows]
    first = place_ref[0] == 0
    zone = place_ref[1]
    local = place_ref[2]
    expert = pl.program_id(0)
    width = out_ref.shape[1]
    acc = None
    for m in range(rows):
        a, b = own[m][0], nbr[m][0]
        w = jnp.concatenate([jnp.where(first, a, b), jnp.where(first, b, a)], axis=0)
        depth = w.shape[0]
        part = jnp.dot(
            x_ref[:, m * depth : (m + 1) * depth], w, preferred_element_type=jnp.float32
        )
        acc = part if acc is None else acc + part
    feats = x_ref.shape[1] - LANES
    lane = lax.broadcasted_iota(jnp.int32, (LANES, width), 0)
    slot = zone * local + expert
    pick = jnp.where((lane == slot) | (lane == slot + LOW), 1.0, 0.0).astype(jnp.bfloat16)
    gate = jnp.dot(x_ref[:, feats:], pick, preferred_element_type=jnp.float32)
    g, u = acc[:, :width], acc[:, width:]
    out_ref[...] = (g / (1.0 + jnp.exp(-g)) * u * gate).astype(jnp.bfloat16)


def up_call(place, x, own, nbr):
    rows = len(own)
    local, depth, cols = own[0].shape
    tokens, lanes = x.shape
    piece = pl.BlockSpec((1, depth, cols), lambda e, p: (e, 0, 0))
    return pl.pallas_call(
        functools.partial(up_kernel, rows),
        grid_spec=pltpu.PrefetchScalarGridSpec(
            num_scalar_prefetch=1,
            grid=(local,),
            in_specs=[pl.BlockSpec((tokens, lanes), lambda e, p: (0, 0))] + [piece] * (2 * rows),
            out_specs=pl.BlockSpec((tokens, cols // 2), lambda e, p: (0, e)),
        ),
        out_shape=jax.ShapeDtypeStruct((tokens, local * cols // 2), jnp.bfloat16),
        compiler_params=pltpu.CompilerParams(vmem_limit_bytes=40 * 1024 * 1024),
        cost_estimate=pl.CostEstimate(
            flops=2 * tokens * lanes * local * cols,
            bytes_accessed=2 * (tokens * lanes + local * lanes * cols),
            transcendentals=tokens * local * cols // 2,
        ),
        name="up",
    )(place, x, *own, *nbr)


def down_kernel(h_ref, w_ref, out_ref):
    w = jnp.concatenate([w_ref[e] for e in range(w_ref.shape[0])], axis=1)
    out_ref[...] = lax.dot_general(
        h_ref[...], w, (((1,), (1,)), ((), ())), preferred_element_type=jnp.float32
    ).astype(out_ref.dtype)


def down_call(hidden, weight):
    tokens, depth = hidden.shape
    local, feats, part = weight.shape
    steps = 2
    return pl.pallas_call(
        down_kernel,
        grid=(steps,),
        in_specs=[
            pl.BlockSpec((tokens // steps, depth), lambda i: (i, 0)),
            pl.BlockSpec((local, feats, part), lambda i: (0, 0, 0)),
        ],
        out_specs=pl.BlockSpec((tokens // steps, feats), lambda i: (i, 0)),
        out_shape=jax.ShapeDtypeStruct((tokens, feats), jnp.bfloat16),
        compiler_params=pltpu.CompilerParams(vmem_limit_bytes=40 * 1024 * 1024),
        cost_estimate=pl.CostEstimate(
            flops=2 * tokens * depth * feats,
            bytes_accessed=2 * (tokens * depth + depth * feats + tokens * feats),
            transcendentals=0,
        ),
        name="down",
    )(hidden, weight)


def body(
    attended,
    residual,
    out_weight,
    norm_gain,
    final_gain,
    routes,
    gate_logits,
    placement,
    gate_up,
    down_weight,
):
    ranks = lax.axis_size("dp")
    zones = lax.axis_size("expert")
    rows = ranks // QUAD
    me = lax.axis_index("dp")
    zone = lax.axis_index("expert")
    core, side, row = me % 2, (me // 2) % 2, me // QUAD
    tok, width = attended.shape
    local, depth, _ = gate_up.shape
    hid = down_weight.shape[2]
    part = hid // QUAD

    def flip(values, bit):
        return lax.ppermute(values, "dp", [(i, i ^ bit) for i in range(ranks)])

    def shift(values, step):
        return lax.ppermute(values, "expert", [(i, (i + step) % zones) for i in range(zones)])

    def columns(values, offset):
        return lax.dynamic_slice_in_dim(values, offset, part, axis=2)

    def quarter(values, c, s):
        blocks = values.shape[2] // hid
        cuts = [columns(values, b * hid + (2 * c + s) * part) for b in range(blocks)]
        return jnp.concatenate(cuts, axis=2) if blocks > 1 else cuts[0]

    def spread(values):
        away = jnp.concatenate([quarter(values, 1 - core, s) for s in range(2)], axis=2)
        got = flip(away, 1)
        size = got.shape[2] // 2
        both = []
        for s in (side, 1 - side):
            mine = quarter(values, core, s)
            theirs = lax.dynamic_slice_in_dim(got, s * size, size, axis=2)
            both.append(
                jnp.where(
                    core == 0,
                    jnp.concatenate([mine, theirs], axis=1),
                    jnp.concatenate([theirs, mine], axis=1),
                )
            )
        return both[0], flip(both[1], 2)

    def widen(pieces):
        bit = 1
        while bit < rows:
            pieces = pieces + [flip(p, bit * QUAD) for p in pieces]
            bit *= 2
        return pieces

    gu_own, gu_nbr = spread(gate_up)
    own, nbr = widen([gu_own]), widen([gu_nbr])
    dn_own, dn_nbr = spread(down_weight)
    halves = [
        widen([jnp.where(side == j, dn_own, dn_nbr)]) for j in range(2)
    ]

    mixed = residual.astype(jnp.float32) + jnp.dot(
        attended, out_weight, preferred_element_type=jnp.float32
    )
    stored = lax.optimization_barrier(mixed.astype(jnp.bfloat16))
    stream_in = stored.astype(jnp.float32)
    normed_in = normalize(stream_in, norm_gain).astype(jnp.bfloat16)
    gates = gate_lanes(slot_gates(routes, gate_logits, placement))
    sent = jnp.concatenate([swap_blocks(normed_in, row, rows), gates], axis=1)

    column = [sent] + [shift(sent, k) for k in range(1, zones)]
    beside = [flip(v, 2) for v in column]
    chip = column + beside
    mate = [flip(v, 1) for v in chip]
    x = jnp.concatenate(chip + mate, axis=0)

    place = jnp.stack([side, zone, jnp.int32(local)]).astype(jnp.int32)
    hidden = up_call(place, x, own, nbr)

    count = zones * tok
    chunks = []
    for m in range(rows):
        for j in range(2):
            partial = down_call(hidden, halves[j][m])
            back = flip(partial[2 * count :], 1)
            summed = (
                partial[: 2 * count].astype(jnp.float32) + back.astype(jnp.float32)
            )
            back = flip(summed[count:].astype(jnp.bfloat16), 2)
            summed = summed[:count] + back.astype(jnp.float32)
            total = summed[:tok]
            for k in range(1, zones):
                piece = summed[k * tok : (k + 1) * tok].astype(jnp.bfloat16)
                total = total + shift(piece, -k).astype(jnp.float32)
            chunks.append(total)
    branch = swap_blocks(jnp.concatenate(chunks, axis=1), row, rows)
    total = stream_in + branch
    return (total.astype(jnp.bfloat16), normalize(total, final_gain).astype(jnp.bfloat16))


def solution(mesh):
    tokens = P(("dp", "expert"), None)
    weights = P("expert", "dp", None)
    return jax.shard_map(
        body,
        mesh=mesh,
        in_specs=(tokens, tokens, P(), P(), P(), tokens, tokens, P(), weights, weights),
        out_specs=(tokens, tokens),
        check_vma=False,
    )
```

```python
import functools

import jax
import jax.numpy as jnp
from jax import lax
from jax.experimental import pallas as pl
from jax.experimental.pallas import tpu as pltpu
from jax.sharding import PartitionSpec as P

EPS = 1e-06
LOGIT_SCALE = 0.5
LANES = 128
LOW = 64
QUAD = 4


def normalize(values, gain):
    return values * lax.rsqrt(jnp.mean(values * values, axis=-1, keepdims=True) + EPS) * gain


def combine_weights(logits):
    scores = jnp.exp(logits.astype(jnp.float32) * LOGIT_SCALE)
    return scores / jnp.sum(scores, axis=-1, keepdims=True)


def slot_gates(routes, logits, placement):
    gates = combine_weights(logits)
    hit = routes[:, :, None] == placement[None, None, :]
    return jnp.sum(jnp.where(hit, gates[:, :, None], 0.0), axis=1)


def gate_lanes(gates):
    high = gates.astype(jnp.bfloat16)
    low = (gates - high.astype(jnp.float32)).astype(jnp.bfloat16)
    pad = ((0, 0), (0, LOW - gates.shape[1]))
    return jnp.concatenate([jnp.pad(high, pad), jnp.pad(low, pad)], axis=1)


def after(values, *others):
    return lax.optimization_barrier((values, *others))[0]


def swap_blocks(values, index, blocks):
    size = values.shape[1] // blocks
    bit = 1
    while bit < blocks:
        swapped = jnp.concatenate(
            [values[:, (m ^ bit) * size : ((m ^ bit) + 1) * size] for m in range(blocks)], axis=1
        )
        values = jnp.where((index & bit) != 0, swapped, values)
        bit *= 2
    return values


def up_kernel(rows, blocks, place_ref, *refs):
    parts, pieces = refs[:blocks], refs[blocks : blocks + QUAD * rows]
    out_ref, x_ref = refs[blocks + QUAD * rows :]
    side, core, zone, local = (place_ref[i] for i in range(4))
    expert = pl.program_id(0)
    width = out_ref.shape[1]

    @pl.when(expert == 0)
    def _():
        at = 0
        for part in parts:
            x_ref[at : at + part.shape[0], :] = part[...]
            at += part.shape[0]

    acc = None
    for m in range(rows):
        own, mate, own_x, mate_x = (pieces[QUAD * m + i][0] for i in range(QUAD))
        near = [jnp.where(core == 0, own, mate), jnp.where(core == 0, mate, own)]
        far = [jnp.where(core == 0, own_x, mate_x), jnp.where(core == 0, mate_x, own_x)]
        order = [jnp.where(side == 0, a, b) for a, b in zip(near + far, far + near)]
        w = jnp.concatenate(order, axis=0)
        depth = w.shape[0]
        part = jnp.dot(
            x_ref[:, m * depth : (m + 1) * depth], w, preferred_element_type=jnp.float32
        )
        acc = part if acc is None else acc + part
    feats = x_ref.shape[1] - LANES
    lane = lax.broadcasted_iota(jnp.int32, (LANES, width), 0)
    slot = zone * local + expert
    pick = jnp.where((lane == slot) | (lane == slot + LOW), 1.0, 0.0).astype(jnp.bfloat16)
    gate = jnp.dot(x_ref[:, feats:], pick, preferred_element_type=jnp.float32)
    g, u = acc[:, :width], acc[:, width:]
    out_ref[...] = (g / (1.0 + jnp.exp(-g)) * u * gate).astype(jnp.bfloat16)


def up_call(place, parts, pieces):
    rows = len(pieces) // QUAD
    local, depth, cols = pieces[0].shape
    tokens, lanes = sum(v.shape[0] for v in parts), parts[0].shape[1]
    piece = pl.BlockSpec((1, depth, cols), lambda e, p: (e, 0, 0))
    return pl.pallas_call(
        functools.partial(up_kernel, rows, len(parts)),
        grid_spec=pltpu.PrefetchScalarGridSpec(
            num_scalar_prefetch=1,
            grid=(local,),
            in_specs=[pl.BlockSpec(v.shape, lambda e, p: (0, 0)) for v in parts]
            + [piece] * len(pieces),
            out_specs=pl.BlockSpec((tokens, cols // 2), lambda e, p: (0, e)),
            scratch_shapes=[pltpu.VMEM((tokens, lanes), jnp.bfloat16)],
        ),
        out_shape=jax.ShapeDtypeStruct((tokens, local * cols // 2), jnp.bfloat16),
        compiler_params=pltpu.CompilerParams(vmem_limit_bytes=48 * 1024 * 1024),
        cost_estimate=pl.CostEstimate(
            flops=2 * tokens * lanes * local * cols,
            bytes_accessed=2 * (tokens * lanes + local * lanes * cols),
            transcendentals=tokens * local * cols // 2,
        ),
        name="up",
    )(place, *parts, *pieces)


def down_kernel(h_ref, w_ref, out_ref):
    w = jnp.concatenate([w_ref[e] for e in range(w_ref.shape[0])], axis=1)
    out_ref[...] = lax.dot_general(
        h_ref[...], w, (((1,), (1,)), ((), ())), preferred_element_type=jnp.float32
    ).astype(out_ref.dtype)


def down_call(hidden, weight):
    tokens, depth = hidden.shape
    local, feats, part = weight.shape
    steps = 2
    return pl.pallas_call(
        down_kernel,
        grid=(steps,),
        in_specs=[
            pl.BlockSpec((tokens // steps, depth), lambda i: (i, 0)),
            pl.BlockSpec((local, feats, part), lambda i: (0, 0, 0)),
        ],
        out_specs=pl.BlockSpec((tokens // steps, feats), lambda i: (i, 0)),
        out_shape=jax.ShapeDtypeStruct((tokens, feats), jnp.bfloat16),
        compiler_params=pltpu.CompilerParams(vmem_limit_bytes=40 * 1024 * 1024),
        cost_estimate=pl.CostEstimate(
            flops=2 * tokens * depth * feats,
            bytes_accessed=2 * (tokens * depth + depth * feats + tokens * feats),
            transcendentals=0,
        ),
        name="down",
    )(hidden, weight)


def body(
    attended,
    residual,
    out_weight,
    norm_gain,
    final_gain,
    routes,
    gate_logits,
    placement,
    gate_up,
    down_weight,
):
    ranks = lax.axis_size("dp")
    zones = lax.axis_size("expert")
    rows = ranks // QUAD
    me = lax.axis_index("dp")
    zone = lax.axis_index("expert")
    core, side, row = me % 2, (me // 2) % 2, me // QUAD
    tok, width = attended.shape
    local, depth, _ = gate_up.shape
    hid = down_weight.shape[2]
    part = hid // QUAD

    def flip(values, bit):
        return lax.ppermute(values, "dp", [(i, i ^ bit) for i in range(ranks)])

    def hop(values, bit):
        return lax.ppermute(values, "expert", [(i, i ^ bit) for i in range(zones)])

    def quarter(values, c, s):
        blocks = values.shape[2] // hid
        cuts = [
            lax.dynamic_slice_in_dim(values, b * hid + (2 * c + s) * part, part, axis=2)
            for b in range(blocks)
        ]
        return jnp.concatenate(cuts, axis=2) if blocks > 1 else cuts[0]

    def from_mate(values):
        away = jnp.concatenate([quarter(values, 1 - core, s) for s in range(2)], axis=2)
        got = flip(away, 1)
        size = got.shape[2] // 2
        return [
            lax.dynamic_slice_in_dim(got, s * size, size, axis=2) for s in (side, 1 - side)
        ]

    def widen(pieces):
        bit = 1
        while bit < rows:
            pieces = pieces + [flip(p, bit * QUAD) for p in pieces]
            bit *= 2
        return pieces

    zone_bits = []
    while 1 << len(zone_bits) < zones:
        zone_bits.insert(0, 1 << len(zone_bits))

    gu_mate, gu_mate_away = from_mate(gate_up)
    gu_own = quarter(gate_up, core, side)
    gu_own_x = flip(quarter(gate_up, core, 1 - side), 2)
    gu_mate_x = flip(gu_mate_away, 2)
    first = widen([gu_own])
    second = widen([gu_mate])
    third = widen([after(gu_own_x, first[-1])])
    fourth = widen([after(gu_mate_x, second[-1])])
    pieces = [p for group in zip(first, second, third, fourth) for p in group]

    mixed = residual.astype(jnp.float32) + jnp.dot(
        attended, out_weight, preferred_element_type=jnp.float32
    )
    stored = lax.optimization_barrier(mixed.astype(jnp.bfloat16))
    stream_in = stored.astype(jnp.float32)
    normed_in = normalize(stream_in, norm_gain).astype(jnp.bfloat16)
    gates = gate_lanes(slot_gates(routes, gate_logits, placement))
    sent = jnp.concatenate([swap_blocks(normed_in, row, rows), gates], axis=1)
    sent = after(sent, gu_own, gu_mate)
    near = sent
    for bit in zone_bits[:-1]:
        near = jnp.concatenate([near, hop(near, bit)], axis=0)
    far = hop(near, zone_bits[-1])
    near_x = flip(near, 2)
    far_x = flip(far, 2)
    chip = [near, far, near_x, far_x]
    parts = chip + [flip(v, 1) for v in chip]

    dn_mate, dn_mate_away = from_mate(down_weight)
    dn_own = quarter(down_weight, core, side)
    dn_away = quarter(down_weight, core, 1 - side)

    def pair(own, mate):
        return jnp.where(
            core == 0,
            jnp.concatenate([own, mate], axis=1),
            jnp.concatenate([mate, own], axis=1),
        )

    dn_near = pair(dn_own, dn_mate)
    dn_far = flip(after(pair(dn_away, dn_mate_away), near_x), 2)
    halves = []
    for j, gate_piece in ((0, third), (1, fourth)):
        half = jnp.where(side == j, dn_near, dn_far)
        halves.append(widen([after(half, gate_piece[-1])]))

    place = jnp.stack([side, core, zone, jnp.int32(local)]).astype(jnp.int32)
    hidden = up_call(place, parts, pieces)

    count = zones * tok
    chunks = []
    for m in range(rows):
        for j in range(2):
            partial = down_call(hidden, halves[j][m])
            back = flip(partial[2 * count :], 1)
            total = partial[: 2 * count].astype(jnp.float32) + back.astype(jnp.float32)
            back = flip(total[count:].astype(jnp.bfloat16), 2)
            total = total[:count] + back.astype(jnp.float32)
            for bit in reversed(zone_bits):
                size = total.shape[0] // 2
                back = hop(total[size:].astype(jnp.bfloat16), bit)
                total = total[:size] + back.astype(jnp.float32)
            chunks.append(total)
    branch = swap_blocks(jnp.concatenate(chunks, axis=1), row, rows)
    total = stream_in + branch
    return (total.astype(jnp.bfloat16), normalize(total, final_gain).astype(jnp.bfloat16))


def solution(mesh):
    tokens = P(("dp", "expert"), None)
    weights = P("expert", "dp", None)
    return jax.shard_map(
        body,
        mesh=mesh,
        in_specs=(tokens, tokens, P(), P(), P(), tokens, tokens, P(), weights, weights),
        out_specs=(tokens, tokens),
        check_vma=False,
    )
```

```python
import functools

import jax
import jax.numpy as jnp
from jax import lax
from jax.experimental import pallas as pl
from jax.experimental.pallas import tpu as pltpu
from jax.sharding import PartitionSpec as P

EPS = 1e-06
LOGIT_SCALE = 0.5
LANES = 128
LOW = 64
QUAD = 4


def normalize(values, gain):
    return values * lax.rsqrt(jnp.mean(values * values, axis=-1, keepdims=True) + EPS) * gain


def after(values, *others):
    return lax.optimization_barrier((values, *others))[0]


def swap_blocks(values, index, blocks):
    size = values.shape[1] // blocks
    bit = 1
    while bit < blocks:
        swapped = jnp.concatenate(
            [values[:, (m ^ bit) * size : ((m ^ bit) + 1) * size] for m in range(blocks)], axis=1
        )
        values = jnp.where((index & bit) != 0, swapped, values)
        bit *= 2
    return values


def swap_lanes(values, index, blocks):
    width = values.shape[1]
    size = width // blocks
    lane = lax.broadcasted_iota(jnp.int32, values.shape, 1)
    bit = 1
    while bit < blocks:
        step = bit * size
        upper = (lane // step) % 2 == 1
        swapped = jnp.where(
            upper, pltpu.roll(values, step, 1), pltpu.roll(values, width - step, 1)
        )
        values = jnp.where((index & bit) != 0, swapped, values)
        bit *= 2
    return values


def front_kernel(
    rows,
    place_ref,
    att_ref,
    res_ref,
    w_ref,
    gain_ref,
    routes_ref,
    logits_ref,
    placed_ref,
    stream_ref,
    sent_ref,
    keep_ref,
):
    step = pl.program_id(0)
    cols = w_ref.shape[1]
    width = att_ref.shape[1]
    mixed = res_ref[...].astype(jnp.float32) + jnp.dot(
        att_ref[...], w_ref[...], preferred_element_type=jnp.float32
    )
    stored = mixed.astype(jnp.bfloat16)
    stream_ref[...] = stored
    keep_ref[:, pl.ds(pl.multiple_of(step * cols, cols), cols)] = stored.astype(jnp.float32)

    @pl.when(step == pl.num_programs(0) - 1)
    def _():
        normed = normalize(keep_ref[...], gain_ref[...])
        sent_ref[:, :width] = swap_lanes(normed, place_ref[4], rows).astype(jnp.bfloat16)
        scores = jnp.exp(logits_ref[...].astype(jnp.float32) * LOGIT_SCALE)
        gates = scores / jnp.sum(scores, axis=1, keepdims=True)
        routes = routes_ref[...]
        spread = jnp.zeros((gates.shape[0], LANES), jnp.float32)
        for k in range(gates.shape[1]):
            hit = routes[:, k : k + 1] == placed_ref[...]
            spread = jnp.where(hit, gates[:, k : k + 1], spread)
        high = spread.astype(jnp.bfloat16).astype(jnp.float32)
        lane = lax.broadcasted_iota(jnp.int32, spread.shape, 1)
        sent_ref[:, width:] = jnp.where(lane < LOW, high, spread - high).astype(jnp.bfloat16)


def front_call(place, rows, attended, residual, weight, gain, routes, logits, placement):
    tok, width = attended.shape
    steps = 4
    cols = width // steps
    padded = jnp.pad(placement, (0, LOW - placement.shape[0]), constant_values=-1)
    placed = jnp.concatenate([padded, padded])[None, :]
    whole = lambda shape: pl.BlockSpec(shape, lambda i, p: (0, 0))
    return pl.pallas_call(
        functools.partial(front_kernel, rows),
        grid_spec=pltpu.PrefetchScalarGridSpec(
            num_scalar_prefetch=1,
            grid=(steps,),
            in_specs=[
                whole((tok, width)),
                pl.BlockSpec((tok, cols), lambda i, p: (0, i)),
                pl.BlockSpec((width, cols), lambda i, p: (0, i)),
                whole((1, width)),
                whole(routes.shape),
                whole(logits.shape),
                whole((1, LANES)),
            ],
            out_specs=[
                pl.BlockSpec((tok, cols), lambda i, p: (0, i)),
                whole((tok, width + LANES)),
            ],
            scratch_shapes=[pltpu.VMEM((tok, width), jnp.float32)],
        ),
        out_shape=[
            jax.ShapeDtypeStruct((tok, width), jnp.bfloat16),
            jax.ShapeDtypeStruct((tok, width + LANES), jnp.bfloat16),
        ],
        compiler_params=pltpu.CompilerParams(vmem_limit_bytes=24 * 1024 * 1024),
        name="front",
    )(place, attended, residual, weight, gain[None, :], routes, logits, placed)


def cut_kernel(part, place_ref, w_ref, *out_refs):
    side, core = place_ref[0], place_ref[1]
    blocks = out_refs[0].shape[2] // part
    targets = [(core, side), (core, 1 - side), (1 - core, side), (1 - core, 1 - side)]
    for out_ref, (c, s) in zip(out_refs, targets):
        for b in range(blocks):
            at = pl.multiple_of(b * QUAD * part + (2 * c + s) * part, part)
            out_ref[:, :, b * part : (b + 1) * part] = w_ref[:, :, pl.ds(at, part)]


def cut_call(place, weight, part):
    local, depth, cols = weight.shape
    out = jax.ShapeDtypeStruct((local, depth, cols // QUAD), jnp.bfloat16)
    return pl.pallas_call(
        functools.partial(cut_kernel, part),
        grid_spec=pltpu.PrefetchScalarGridSpec(
            num_scalar_prefetch=1,
            grid=(local,),
            in_specs=[pl.BlockSpec((1, depth, cols), lambda e, p: (e, 0, 0))],
            out_specs=[pl.BlockSpec((1, depth, cols // QUAD), lambda e, p: (e, 0, 0))] * QUAD,
        ),
        out_shape=[out] * QUAD,
        name="cut",
    )(place, weight)


def up_kernel(rows, blocks, place_ref, *refs):
    parts, pieces = refs[:blocks], refs[blocks : blocks + QUAD * rows]
    out_ref, x_ref = refs[blocks + QUAD * rows :]
    side, core, zone, local = (place_ref[i] for i in range(4))
    expert = pl.program_id(0)
    width = out_ref.shape[1]

    @pl.when(expert == 0)
    def _():
        at = 0
        for part in parts:
            x_ref[at : at + part.shape[0], :] = part[...]
            at += part.shape[0]

    acc = None
    for m in range(rows):
        own, mate, own_x, mate_x = (pieces[QUAD * m + i][0] for i in range(QUAD))
        near = [jnp.where(core == 0, own, mate), jnp.where(core == 0, mate, own)]
        far = [jnp.where(core == 0, own_x, mate_x), jnp.where(core == 0, mate_x, own_x)]
        order = [jnp.where(side == 0, a, b) for a, b in zip(near + far, far + near)]
        w = jnp.concatenate(order, axis=0)
        depth = w.shape[0]
        part = jnp.dot(
            x_ref[:, m * depth : (m + 1) * depth], w, preferred_element_type=jnp.float32
        )
        acc = part if acc is None else acc + part
    feats = x_ref.shape[1] - LANES
    lane = lax.broadcasted_iota(jnp.int32, (LANES, width), 0)
    slot = zone * local + expert
    pick = jnp.where((lane == slot) | (lane == slot + LOW), 1.0, 0.0).astype(jnp.bfloat16)
    gate = jnp.dot(x_ref[:, feats:], pick, preferred_element_type=jnp.float32)
    g, u = acc[:, :width], acc[:, width:]
    out_ref[...] = (g / (1.0 + jnp.exp(-g)) * u * gate).astype(jnp.bfloat16)


def up_call(place, parts, pieces):
    rows = len(pieces) // QUAD
    local, depth, cols = pieces[0].shape
    tokens, lanes = sum(v.shape[0] for v in parts), parts[0].shape[1]
    piece = pl.BlockSpec((1, depth, cols), lambda e, p: (e, 0, 0))
    return pl.pallas_call(
        functools.partial(up_kernel, rows, len(parts)),
        grid_spec=pltpu.PrefetchScalarGridSpec(
            num_scalar_prefetch=1,
            grid=(local,),
            in_specs=[pl.BlockSpec(v.shape, lambda e, p: (0, 0)) for v in parts]
            + [piece] * len(pieces),
            out_specs=pl.BlockSpec((tokens, cols // 2), lambda e, p: (0, e)),
            scratch_shapes=[pltpu.VMEM((tokens, lanes), jnp.bfloat16)],
        ),
        out_shape=jax.ShapeDtypeStruct((tokens, local * cols // 2), jnp.bfloat16),
        compiler_params=pltpu.CompilerParams(vmem_limit_bytes=48 * 1024 * 1024),
        cost_estimate=pl.CostEstimate(
            flops=2 * tokens * lanes * local * cols,
            bytes_accessed=2 * (tokens * lanes + local * lanes * cols),
            transcendentals=tokens * local * cols // 2,
        ),
        name="up",
    )(place, *parts, *pieces)


def down_kernel(place_ref, h_ref, near_ref, far_ref, send_ref, keep_ref):
    side = place_ref[0]
    feats = near_ref.shape[1]
    parts = []
    for e in range(near_ref.shape[0]):
        near, far = near_ref[e], far_ref[e]
        parts.append([jnp.where(side == 0, near, far), jnp.where(side == 0, far, near)])

    def times(j):
        w = jnp.concatenate([p[j] for p in parts], axis=1)
        return lax.dot_general(
            h_ref[...], w, (((1,), (1,)), ((), ())), preferred_element_type=jnp.float32
        )

    @pl.when(pl.program_id(0) == 0)
    def _():
        for j in range(2):
            send_ref[:, j * feats : (j + 1) * feats] = times(j).astype(send_ref.dtype)

    @pl.when(pl.program_id(0) == 1)
    def _():
        for j in range(2):
            keep_ref[:, j * feats : (j + 1) * feats] = times(j)


def down_call(place, hidden, near, far):
    tokens, depth = hidden.shape
    local, feats, part = near.shape
    half = tokens // 2
    whole = pl.BlockSpec((local, feats, part), lambda i, p: (0, 0, 0))
    out = pl.BlockSpec((half, 2 * feats), lambda i, p: (0, 0))
    return pl.pallas_call(
        down_kernel,
        grid_spec=pltpu.PrefetchScalarGridSpec(
            num_scalar_prefetch=1,
            grid=(2,),
            in_specs=[pl.BlockSpec((half, depth), lambda i, p: (1 - i, 0)), whole, whole],
            out_specs=[out, out],
        ),
        out_shape=[
            jax.ShapeDtypeStruct((half, 2 * feats), jnp.bfloat16),
            jax.ShapeDtypeStruct((half, 2 * feats), jnp.float32),
        ],
        compiler_params=pltpu.CompilerParams(vmem_limit_bytes=40 * 1024 * 1024),
        cost_estimate=pl.CostEstimate(
            flops=4 * tokens * depth * feats,
            bytes_accessed=2 * (tokens * depth + 2 * depth * feats + 3 * tokens * feats),
            transcendentals=0,
        ),
        name="down",
    )(place, hidden, near, far)


def body(
    attended,
    residual,
    out_weight,
    norm_gain,
    final_gain,
    routes,
    gate_logits,
    placement,
    gate_up,
    down_weight,
):
    ranks = lax.axis_size("dp")
    zones = lax.axis_size("expert")
    rows = ranks // QUAD
    me = lax.axis_index("dp")
    zone = lax.axis_index("expert")
    core, side, row = me % 2, (me // 2) % 2, me // QUAD
    tok, width = attended.shape
    local, depth, _ = gate_up.shape
    hid = down_weight.shape[2]
    part = hid // QUAD

    def flip(values, bit):
        return lax.ppermute(values, "dp", [(i, i ^ bit) for i in range(ranks)])

    def hop(values, bit):
        return lax.ppermute(values, "expert", [(i, i ^ bit) for i in range(zones)])

    def widen(pieces):
        bit = 1
        while bit < rows:
            pieces = pieces + [flip(p, bit * QUAD) for p in pieces]
            bit *= 2
        return pieces

    zone_bits = []
    while 1 << len(zone_bits) < zones:
        zone_bits.insert(0, 1 << len(zone_bits))

    place = jnp.stack([side, core, zone, jnp.int32(local), row]).astype(jnp.int32)

    gu_own, gu_away, gu_to_mate, gu_to_mate_away = cut_call(place, gate_up, part)
    stored, sent = front_call(
        place, rows, after(attended, gu_own), residual, out_weight, norm_gain, routes, gate_logits, placement
    )
    stream_in = stored.astype(jnp.float32)
    gu_own_x = flip(gu_away, 2)
    first = widen([gu_own])
    gu_mate, gu_mate_away = flip(gu_to_mate, 1), flip(gu_to_mate_away, 1)
    gu_mate_x = flip(after(gu_mate_away, gu_own_x, first[-1]), 2)
    second = widen([after(gu_mate, first[-1], sent)])
    third = widen([after(gu_own_x, second[-1])])
    fourth = widen([after(gu_mate_x, third[-1])])
    pieces = [p for group in zip(first, second, third, fourth) for p in group]

    near = sent
    for bit in zone_bits[:-1]:
        near = jnp.concatenate([near, hop(near, bit)], axis=0)
    far = hop(near, zone_bits[-1])
    near_x = flip(after(near, gu_mate_x, second[-1]), 2)
    far_x = flip(after(far, near_x, third[-1]), 2)
    chip = [near, after(far, fourth[-1]), near_x, after(far_x, fourth[-1])]
    parts = chip + [flip(v, 1) for v in chip]

    dn_own, dn_away, dn_to_mate, dn_to_mate_away = cut_call(place, down_weight, part)
    dn_mate, dn_mate_away = flip(dn_to_mate, 1), flip(dn_to_mate_away, 1)

    def pair(own, mate):
        return jnp.where(
            core == 0,
            jnp.concatenate([own, mate], axis=1),
            jnp.concatenate([mate, own], axis=1),
        )

    dn_near = pair(dn_own, dn_mate)
    dn_far = flip(after(pair(dn_away, dn_mate_away), far_x), 2)
    dn_nears = widen([after(dn_near, fourth[-1])])
    hidden = after(up_call(place, parts, pieces), dn_nears[-1])
    dn_fars = widen([after(dn_far, dn_nears[-1], hidden)])

    count = zones * tok
    sums = []
    for m in range(rows):
        ready = after(hidden, *(v[1] for v in sums[-2:-1]))
        send, keep = down_call(place, ready, dn_nears[m], dn_fars[m])
        back = flip(send, 1)
        feats = send.shape[1] // 2
        for j in range(2):
            cols = slice(j * feats, (j + 1) * feats)
            total = keep[:, cols] + back[:, cols].astype(jnp.float32)
            away = total[count:].astype(jnp.bfloat16)
            crossed = flip(after(away, *(v[1] for v in sums[-2:-1])), 2)
            sums.append((total[:count], crossed))
    merged = [
        (jnp.concatenate([a[0], b[0]], axis=1), jnp.concatenate([a[1], b[1]], axis=1))
        for a, b in zip(sums[:-2:2], sums[1:-2:2])
    ]
    chunks = []
    for i, (total, crossed) in enumerate(merged + sums[-2:]):
        total = total + crossed.astype(jnp.float32)
        for bit in reversed(zone_bits):
            size = total.shape[0] // 2
            away = total[size:].astype(jnp.bfloat16)
            if i < len(merged) and bit == zone_bits[0]:
                away = after(away, sums[-2][1])
            total = total[:size] + hop(away, bit).astype(jnp.float32)
        chunks.append(total)
    branch = swap_blocks(jnp.concatenate(chunks, axis=1), row, rows)
    total = stream_in + branch
    return (total.astype(jnp.bfloat16), normalize(total, final_gain).astype(jnp.bfloat16))


def solution(mesh):
    tokens = P(("dp", "expert"), None)
    weights = P("expert", "dp", None)
    return jax.shard_map(
        body,
        mesh=mesh,
        in_specs=(tokens, tokens, P(), P(), P(), tokens, tokens, P(), weights, weights),
        out_specs=(tokens, tokens),
        check_vma=False,
    )
```

```python
import functools

import jax
import jax.numpy as jnp
from jax import lax
from jax.experimental import pallas as pl
from jax.experimental.pallas import tpu as pltpu
from jax.sharding import PartitionSpec as P

EPS = 1e-06
LOGIT_SCALE = 0.5
LANES = 128
LOW = 64
QUAD = 4


def normalize(values, gain):
    return values * lax.rsqrt(jnp.mean(values * values, axis=-1, keepdims=True) + EPS) * gain


def after(values, *others):
    return lax.optimization_barrier((values, *others))[0]


def swap_blocks(values, index, blocks):
    size = values.shape[1] // blocks
    bit = 1
    while bit < blocks:
        swapped = jnp.concatenate(
            [values[:, (m ^ bit) * size : ((m ^ bit) + 1) * size] for m in range(blocks)], axis=1
        )
        values = jnp.where((index & bit) != 0, swapped, values)
        bit *= 2
    return values


def swap_lanes(values, index, blocks):
    width = values.shape[1]
    size = width // blocks
    lane = lax.broadcasted_iota(jnp.int32, values.shape, 1)
    bit = 1
    while bit < blocks:
        step = bit * size
        upper = (lane // step) % 2 == 1
        swapped = jnp.where(
            upper, pltpu.roll(values, step, 1), pltpu.roll(values, width - step, 1)
        )
        values = jnp.where((index & bit) != 0, swapped, values)
        bit *= 2
    return values


def front_kernel(
    rows,
    place_ref,
    att_ref,
    res_ref,
    w_ref,
    gain_ref,
    routes_ref,
    logits_ref,
    placed_ref,
    stream_ref,
    sent_ref,
    keep_ref,
):
    step = pl.program_id(0)
    cols = w_ref.shape[1]
    width = att_ref.shape[1]
    mixed = res_ref[...].astype(jnp.float32) + jnp.dot(
        att_ref[...], w_ref[...], preferred_element_type=jnp.float32
    )
    stored = mixed.astype(jnp.bfloat16)
    stream_ref[...] = stored
    keep_ref[:, pl.ds(pl.multiple_of(step * cols, cols), cols)] = stored.astype(jnp.float32)

    @pl.when(step == pl.num_programs(0) - 1)
    def _():
        normed = normalize(keep_ref[...], gain_ref[...])
        sent_ref[:, :width] = swap_lanes(normed, place_ref[4], rows).astype(jnp.bfloat16)
        scores = jnp.exp(logits_ref[...].astype(jnp.float32) * LOGIT_SCALE)
        gates = scores / jnp.sum(scores, axis=1, keepdims=True)
        routes = routes_ref[...]
        spread = jnp.zeros((gates.shape[0], LANES), jnp.float32)
        for k in range(gates.shape[1]):
            hit = routes[:, k : k + 1] == placed_ref[...]
            spread = jnp.where(hit, gates[:, k : k + 1], spread)
        high = spread.astype(jnp.bfloat16).astype(jnp.float32)
        lane = lax.broadcasted_iota(jnp.int32, spread.shape, 1)
        sent_ref[:, width:] = jnp.where(lane < LOW, high, spread - high).astype(jnp.bfloat16)


def front_call(place, rows, attended, residual, weight, gain, routes, logits, placement):
    tok, width = attended.shape
    steps = 4
    cols = width // steps
    padded = jnp.pad(placement, (0, LOW - placement.shape[0]), constant_values=-1)
    placed = jnp.concatenate([padded, padded])[None, :]
    whole = lambda shape: pl.BlockSpec(shape, lambda i, p: (0, 0))
    return pl.pallas_call(
        functools.partial(front_kernel, rows),
        grid_spec=pltpu.PrefetchScalarGridSpec(
            num_scalar_prefetch=1,
            grid=(steps,),
            in_specs=[
                whole((tok, width)),
                pl.BlockSpec((tok, cols), lambda i, p: (0, i)),
                pl.BlockSpec((width, cols), lambda i, p: (0, i)),
                whole((1, width)),
                whole(routes.shape),
                whole(logits.shape),
                whole((1, LANES)),
            ],
            out_specs=[
                pl.BlockSpec((tok, cols), lambda i, p: (0, i)),
                whole((tok, width + LANES)),
            ],
            scratch_shapes=[pltpu.VMEM((tok, width), jnp.float32)],
        ),
        out_shape=[
            jax.ShapeDtypeStruct((tok, width), jnp.bfloat16),
            jax.ShapeDtypeStruct((tok, width + LANES), jnp.bfloat16),
        ],
        compiler_params=pltpu.CompilerParams(vmem_limit_bytes=24 * 1024 * 1024),
        name="front",
    )(place, attended, residual, weight, gain[None, :], routes, logits, placed)


def cut_kernel(part, place_ref, w_ref, *out_refs):
    side, core = place_ref[0], place_ref[1]
    blocks = out_refs[0].shape[2] // part
    targets = [(core, side), (core, 1 - side), (1 - core, side), (1 - core, 1 - side)]
    for out_ref, (c, s) in zip(out_refs, targets):
        for b in range(blocks):
            at = pl.multiple_of(b * QUAD * part + (2 * c + s) * part, part)
            out_ref[:, :, b * part : (b + 1) * part] = w_ref[:, :, pl.ds(at, part)]


def cut_call(place, weight, part):
    local, depth, cols = weight.shape
    out = jax.ShapeDtypeStruct((local, depth, cols // QUAD), jnp.bfloat16)
    return pl.pallas_call(
        functools.partial(cut_kernel, part),
        grid_spec=pltpu.PrefetchScalarGridSpec(
            num_scalar_prefetch=1,
            grid=(1,),
            in_specs=[pl.BlockSpec((local, depth, cols), lambda i, p: (0, 0, 0))],
            out_specs=[pl.BlockSpec((local, depth, cols // QUAD), lambda i, p: (0, 0, 0))] * QUAD,
        ),
        out_shape=[out] * QUAD,
        compiler_params=pltpu.CompilerParams(vmem_limit_bytes=24 * 1024 * 1024),
        name="cut",
    )(place, weight)


def up_kernel(rows, blocks, place_ref, *refs):
    parts, pieces = refs[:blocks], refs[blocks : blocks + 2 * QUAD * rows]
    out_ref, x_ref = refs[blocks + 2 * QUAD * rows :]
    side, core, zone, local = (place_ref[i] for i in range(4))
    expert = pl.program_id(0)
    width = out_ref.shape[1]
    part = width // 2

    @pl.when(expert == 0)
    def _():
        at = 0
        for block in parts:
            x_ref[at : at + block.shape[0], :] = block[...]
            at += block.shape[0]

    def ordered(group):
        order = []
        for m in range(rows):
            own, mate, own_x, mate_x = (group[QUAD * m + i][0] for i in range(QUAD))
            near = [jnp.where(core == 0, own, mate), jnp.where(core == 0, mate, own)]
            far = [jnp.where(core == 0, own_x, mate_x), jnp.where(core == 0, mate_x, own_x)]
            order += [jnp.where(side == 0, a, b) for a, b in zip(near + far, far + near)]
        return jnp.concatenate(order, axis=0)

    mine, other = ordered(pieces[: QUAD * rows]), ordered(pieces[QUAD * rows :])
    w = jnp.concatenate(
        [mine[:, :part], other[:, :part], mine[:, part:], other[:, part:]], axis=1
    )
    feats = x_ref.shape[1] - LANES
    lane = lax.broadcasted_iota(jnp.int32, (LANES, width), 0)
    slot = zone * local + expert
    pick = jnp.where((lane == slot) | (lane == slot + LOW), 1.0, 0.0).astype(jnp.bfloat16)
    acc = jnp.dot(x_ref[:, :feats], w, preferred_element_type=jnp.float32)
    gate = jnp.dot(x_ref[:, feats:], pick, preferred_element_type=jnp.float32)
    g, u = acc[:, :width], acc[:, width:]
    out_ref[...] = (g / (1.0 + jnp.exp(-g)) * u * gate).astype(jnp.bfloat16)


def up_call(place, parts, mine, other):
    rows = len(mine) // QUAD
    local, depth, cols = mine[0].shape
    tokens, lanes = sum(v.shape[0] for v in parts), parts[0].shape[1]
    piece = pl.BlockSpec((1, depth, cols), lambda e, p: (e, 0, 0))
    return pl.pallas_call(
        functools.partial(up_kernel, rows, len(parts)),
        grid_spec=pltpu.PrefetchScalarGridSpec(
            num_scalar_prefetch=1,
            grid=(local,),
            in_specs=[pl.BlockSpec(v.shape, lambda e, p: (0, 0)) for v in parts]
            + [piece] * (2 * len(mine)),
            out_specs=pl.BlockSpec((tokens, cols), lambda e, p: (0, e)),
            scratch_shapes=[pltpu.VMEM((tokens, lanes), jnp.bfloat16)],
        ),
        out_shape=jax.ShapeDtypeStruct((tokens, local * cols), jnp.bfloat16),
        compiler_params=pltpu.CompilerParams(vmem_limit_bytes=48 * 1024 * 1024),
        cost_estimate=pl.CostEstimate(flops=1, bytes_accessed=1, transcendentals=0),
        name="up",
    )(place, *parts, *mine, *other)


def down_kernel(start, place_ref, h_ref, near_ref, near_other_ref, far_ref, far_other_ref, *out_refs):
    first = place_ref[0] == 0
    feats = near_ref.shape[1]
    order = [[], []]
    for e in range(near_ref.shape[0]):
        for near, far in ((near_ref[e], far_ref[e]), (near_other_ref[e], far_other_ref[e])):
            order[0].append(jnp.where(first, near, far))
            order[1].append(jnp.where(first, far, near))
    for j in range(2):
        partial = lax.dot_general(
            h_ref[start : start + out_refs[0].shape[0], :],
            jnp.concatenate(order[j], axis=1),
            (((1,), (1,)), ((), ())),
            preferred_element_type=jnp.float32,
        )
        if len(out_refs) == 2:
            out_refs[j][...] = partial.astype(out_refs[j].dtype)
        else:
            out_refs[0][:, j * feats : (j + 1) * feats] = partial


def down_call(place, hidden, near, far, send):
    tokens = hidden.shape[0] // 2
    feats = near[0].shape[1]
    if send:
        out = [jax.ShapeDtypeStruct((tokens, feats), jnp.bfloat16)] * 2
    else:
        out = jax.ShapeDtypeStruct((tokens, 2 * feats), jnp.float32)
    return pl.pallas_call(
        functools.partial(down_kernel, tokens if send else 0),
        in_specs=[pl.BlockSpec(memory_space=pltpu.SMEM)]
        + [pl.BlockSpec(memory_space=pltpu.VMEM)] * 5,
        out_specs=[pl.BlockSpec(memory_space=pltpu.VMEM)] * 2
        if send
        else pl.BlockSpec(memory_space=pltpu.VMEM),
        out_shape=out,
        compiler_params=pltpu.CompilerParams(vmem_limit_bytes=40 * 1024 * 1024),
        cost_estimate=pl.CostEstimate(flops=1, bytes_accessed=1, transcendentals=0),
        name="down",
    )(place, hidden, *near, *far)


def body(
    attended,
    residual,
    out_weight,
    norm_gain,
    final_gain,
    routes,
    gate_logits,
    placement,
    gate_up,
    down_weight,
):
    ranks = lax.axis_size("dp")
    zones = lax.axis_size("expert")
    rows = ranks // QUAD
    me = lax.axis_index("dp")
    zone = lax.axis_index("expert")
    core, side, row = me % 2, (me // 2) % 2, me // QUAD
    tok, width = attended.shape
    local, depth, _ = gate_up.shape
    hid = down_weight.shape[2]
    part = hid // QUAD

    def flip(values, bit):
        return lax.ppermute(values, "dp", [(i, i ^ bit) for i in range(ranks)])

    def hop(values, bit):
        return lax.ppermute(values, "expert", [(i, i ^ bit) for i in range(zones)])

    def widen(pieces):
        bit = 1
        while bit < rows:
            pieces = pieces + [flip(p, bit * QUAD) for p in pieces]
            bit *= 2
        return pieces

    zone_bits = []
    while 1 << len(zone_bits) < zones:
        zone_bits.insert(0, 1 << len(zone_bits))

    place = jnp.stack([side, core, zone, jnp.int32(local), row]).astype(jnp.int32)

    gu_own, gu_away, gu_to_mate, gu_to_mate_away = cut_call(place, gate_up, part)
    stored, sent = front_call(
        place, rows, after(attended, gu_own), residual, out_weight, norm_gain, routes, gate_logits, placement
    )
    stream_in = stored.astype(jnp.float32)
    gu_own_x = flip(gu_away, 2)
    first = widen([gu_own])
    gu_mate, gu_mate_away = flip(gu_to_mate, 1), flip(gu_to_mate_away, 1)
    gu_mate_x = flip(after(gu_mate_away, gu_own_x, first[-1]), 2)
    second = widen([after(gu_mate, first[-1], sent)])
    third = widen([after(gu_own_x, second[-1])])
    fourth = widen([after(gu_mate_x, third[-1])])
    mine = [p for group in zip(first, second, third, fourth) for p in group]
    shared = [flip(gu_own, 1), flip(gu_own_x, 1), flip(gu_mate_x, 1)]
    firsts, seconds, thirds, fourths = (
        [flip(p, 1) for p in group[1:]] for group in (first, second, third, fourth)
    )
    other = [gu_to_mate, shared[0], shared[2], shared[1]]
    for group in zip(seconds, firsts, fourths, thirds):
        other += group

    dn_own, dn_away, dn_to_mate, dn_to_mate_away = cut_call(place, after(down_weight, first[-1]), part)
    dn_mate, dn_mate_away = flip(dn_to_mate, 1), flip(dn_to_mate_away, 1)

    def pair(own, mate):
        return jnp.where(
            core == 0,
            jnp.concatenate([own, mate], axis=1),
            jnp.concatenate([mate, own], axis=1),
        )

    dn_near = pair(dn_own, dn_mate)
    dn_away = pair(dn_away, dn_mate_away)
    near = sent
    for bit in zone_bits[:-1]:
        near = jnp.concatenate([near, hop(near, bit)], axis=0)
    far = hop(after(near, second[-1]), zone_bits[-1])
    near_x = flip(
        after(near, gu_mate_x, second[-1], dn_near, dn_away, shared[0], shared[1], *firsts), 2
    )
    far_x = flip(after(far, near_x, third[-1], shared[2], *seconds), 2)
    dn_far = flip(after(dn_away, far_x, *thirds), 2)
    hidden = up_call(place, [near, far, near_x, far_x], mine, other)
    dn_nears = widen([after(dn_near, fourth[-1])])
    dn_fars = widen([after(dn_far, dn_nears[-1])])
    dn_nears = [(v, flip(after(v, hidden), 1)) for v in dn_nears]
    dn_fars = [(v, flip(after(v, hidden), 1)) for v in dn_fars]

    sums = []
    for m in range(rows):
        ready = after(hidden, *(v[1] for v in sums[-2:-1]))
        sends = down_call(place, ready, dn_nears[m], dn_fars[m], True)
        keep = down_call(place, after(hidden, sends[0]), dn_nears[m], dn_fars[m], False)
        feats = keep.shape[1] // 2
        for j in range(2):
            crossed = flip(after(sends[j], *(v[1] for v in sums[-1:])), 2)
            sums.append((keep[:, j * feats : (j + 1) * feats], crossed))
    merged = [
        (jnp.concatenate([a[0], b[0]], axis=1), jnp.concatenate([a[1], b[1]], axis=1))
        for a, b in zip(sums[:-2:2], sums[1:-2:2])
    ]
    chunks = []
    for i, (total, crossed) in enumerate(merged + sums[-2:]):
        total = total + crossed.astype(jnp.float32)
        for bit in reversed(zone_bits):
            size = total.shape[0] // 2
            moved = total[size:].astype(jnp.bfloat16)
            if i < len(merged) and bit == zone_bits[0]:
                moved = after(moved, sums[-2][1])
            total = total[:size] + hop(moved, bit).astype(jnp.float32)
        chunks.append(total)
    branch = swap_blocks(jnp.concatenate(chunks, axis=1), row, rows)
    total = stream_in + branch
    return (total.astype(jnp.bfloat16), normalize(total, final_gain).astype(jnp.bfloat16))


def solution(mesh):
    tokens = P(("dp", "expert"), None)
    weights = P("expert", "dp", None)
    return jax.shard_map(
        body,
        mesh=mesh,
        in_specs=(tokens, tokens, P(), P(), P(), tokens, tokens, P(), weights, weights),
        out_specs=(tokens, tokens),
        check_vma=False,
    )
```

```python
import functools

import jax
import jax.numpy as jnp
from jax import lax
from jax.experimental import pallas as pl
from jax.experimental.pallas import tpu as pltpu
from jax.sharding import PartitionSpec as P

EPS = 1e-06
LOGIT_SCALE = 0.5
LANES = 128
LOW = 64
QUAD = 4


def normalize(values, gain):
    return values * lax.rsqrt(jnp.mean(values * values, axis=-1, keepdims=True) + EPS) * gain


def after(values, *others):
    return lax.optimization_barrier((values, *others))[0]


def after_all(values, *others):
    return lax.optimization_barrier((*values, *others))[: len(values)]


def swap_blocks(values, index, blocks):
    size = values.shape[1] // blocks
    bit = 1
    while bit < blocks:
        swapped = jnp.concatenate(
            [values[:, (m ^ bit) * size : ((m ^ bit) + 1) * size] for m in range(blocks)], axis=1
        )
        values = jnp.where((index & bit) != 0, swapped, values)
        bit *= 2
    return values


def swap_lanes(values, index, blocks):
    width = values.shape[1]
    size = width // blocks
    lane = lax.broadcasted_iota(jnp.int32, values.shape, 1)
    bit = 1
    while bit < blocks:
        step = bit * size
        upper = (lane // step) % 2 == 1
        swapped = jnp.where(
            upper, pltpu.roll(values, step, 1), pltpu.roll(values, width - step, 1)
        )
        values = jnp.where((index & bit) != 0, swapped, values)
        bit *= 2
    return values


def front_kernel(
    rows,
    place_ref,
    att_ref,
    res_ref,
    w_ref,
    gain_ref,
    routes_ref,
    logits_ref,
    placed_ref,
    stream_ref,
    head_ref,
    tail_ref,
    keep_ref,
):
    step = pl.program_id(0)
    cols = w_ref.shape[1]
    width = att_ref.shape[1]
    mixed = res_ref[...].astype(jnp.float32) + jnp.dot(
        att_ref[...], w_ref[...], preferred_element_type=jnp.float32
    )
    stored = mixed.astype(jnp.bfloat16)
    stream_ref[...] = stored
    keep_ref[:, pl.ds(pl.multiple_of(step * cols, cols), cols)] = stored.astype(jnp.float32)

    @pl.when(step == pl.num_programs(0) - 1)
    def _():
        normed = normalize(keep_ref[...], gain_ref[...])
        moved = swap_lanes(normed, place_ref[4], rows).astype(jnp.bfloat16)
        half = width // 2
        head_ref[:, :half] = moved[:, :half]
        tail_ref[...] = moved[:, half:]
        scores = jnp.exp(logits_ref[...].astype(jnp.float32) * LOGIT_SCALE)
        gates = scores / jnp.sum(scores, axis=1, keepdims=True)
        routes = routes_ref[...]
        spread = jnp.zeros((gates.shape[0], LANES), jnp.float32)
        for k in range(gates.shape[1]):
            hit = routes[:, k : k + 1] == placed_ref[...]
            spread = jnp.where(hit, gates[:, k : k + 1], spread)
        high = spread.astype(jnp.bfloat16).astype(jnp.float32)
        lane = lax.broadcasted_iota(jnp.int32, spread.shape, 1)
        head_ref[:, half:] = jnp.where(lane < LOW, high, spread - high).astype(jnp.bfloat16)


def front_call(place, rows, attended, residual, weight, gain, routes, logits, placement):
    tok, width = attended.shape
    steps = 4
    cols = width // steps
    padded = jnp.pad(placement, (0, LOW - placement.shape[0]), constant_values=-1)
    placed = jnp.concatenate([padded, padded])[None, :]
    whole = lambda shape: pl.BlockSpec(shape, lambda i, p: (0, 0))
    return pl.pallas_call(
        functools.partial(front_kernel, rows),
        grid_spec=pltpu.PrefetchScalarGridSpec(
            num_scalar_prefetch=1,
            grid=(steps,),
            in_specs=[
                whole((tok, width)),
                pl.BlockSpec((tok, cols), lambda i, p: (0, i)),
                pl.BlockSpec((width, cols), lambda i, p: (0, i)),
                whole((1, width)),
                whole(routes.shape),
                whole(logits.shape),
                whole((1, LANES)),
            ],
            out_specs=[
                pl.BlockSpec((tok, cols), lambda i, p: (0, i)),
                whole((tok, width // 2 + LANES)),
                whole((tok, width // 2)),
            ],
            scratch_shapes=[pltpu.VMEM((tok, width), jnp.float32)],
        ),
        out_shape=[
            jax.ShapeDtypeStruct((tok, width), jnp.bfloat16),
            jax.ShapeDtypeStruct((tok, width // 2 + LANES), jnp.bfloat16),
            jax.ShapeDtypeStruct((tok, width // 2), jnp.bfloat16),
        ],
        compiler_params=pltpu.CompilerParams(vmem_limit_bytes=24 * 1024 * 1024),
        name="front",
    )(place, attended, residual, weight, gain[None, :], routes, logits, placed)


def cut_kernel(part, place_ref, w_ref, *out_refs):
    side, core = place_ref[0], place_ref[1]
    blocks = out_refs[0].shape[2] // part
    targets = [(core, side), (core, 1 - side), (1 - core, side), (1 - core, 1 - side)]
    for out_ref, (c, s) in zip(out_refs, targets):
        for b in range(blocks):
            at = pl.multiple_of(b * QUAD * part + (2 * c + s) * part, part)
            out_ref[:, :, b * part : (b + 1) * part] = w_ref[:, :, pl.ds(at, part)]


def cut_call(place, weight, part):
    local, depth, cols = weight.shape
    out = jax.ShapeDtypeStruct((local, depth, cols // QUAD), jnp.bfloat16)
    return pl.pallas_call(
        functools.partial(cut_kernel, part),
        grid_spec=pltpu.PrefetchScalarGridSpec(
            num_scalar_prefetch=1,
            grid=(1,),
            in_specs=[pl.BlockSpec((local, depth, cols), lambda i, p: (0, 0, 0))],
            out_specs=[pl.BlockSpec((local, depth, cols // QUAD), lambda i, p: (0, 0, 0))] * QUAD,
        ),
        out_shape=[out] * QUAD,
        compiler_params=pltpu.CompilerParams(vmem_limit_bytes=24 * 1024 * 1024),
        name="cut",
    )(place, weight)


def up_kernel(rows, heads, tails, tok, place_ref, *refs):
    head, tail = refs[:heads], refs[heads : heads + tails]
    pieces = refs[heads + tails : heads + tails + 2 * QUAD * rows]
    out_ref, x_ref = refs[heads + tails + 2 * QUAD * rows :]
    side, core, zone = (place_ref[i] for i in range(3))
    local, _, width = pieces[0].shape
    part = width // 2
    half = tail[0].shape[1]
    blocks = x_ref.shape[0] // tok

    at = 0
    for block in head:
        some = slice(at, at + block.shape[0])
        x_ref[some, :half] = block[:, :half]
        x_ref[some, 2 * half :] = block[:, half:]
        at += block.shape[0]
    at = 0
    for block in tail:
        for i in range(block.shape[0] // tok):
            to = (at % 2) * (blocks // 2) + at // 2
            x_ref[to * tok : (to + 1) * tok, half : 2 * half] = block[i * tok : (i + 1) * tok, :]
            at += 1

    def ordered(group, e):
        order = []
        for m in range(rows):
            own, mate, own_x, mate_x = (group[QUAD * m + i][e] for i in range(QUAD))
            near = [jnp.where(core == 0, own, mate), jnp.where(core == 0, mate, own)]
            far = [jnp.where(core == 0, own_x, mate_x), jnp.where(core == 0, mate_x, own_x)]
            order += [jnp.where(side == 0, a, b) for a, b in zip(near + far, far + near)]
        return jnp.concatenate(order, axis=0)

    lane = lax.broadcasted_iota(jnp.int32, (LANES, width), 0)
    for e in range(local):
        mine, other = ordered(pieces[: QUAD * rows], e), ordered(pieces[QUAD * rows :], e)
        w = jnp.concatenate(
            [mine[:, :part], other[:, :part], mine[:, part:], other[:, part:]], axis=1
        )
        slot = zone * local + e
        pick = jnp.where((lane == slot) | (lane == slot + LOW), 1.0, 0.0).astype(jnp.bfloat16)
        acc = jnp.dot(x_ref[:, : 2 * half], w, preferred_element_type=jnp.float32)
        gate = jnp.dot(x_ref[:, 2 * half :], pick, preferred_element_type=jnp.float32)
        g, u = acc[:, :width], acc[:, width:]
        out_ref[:, e * width : (e + 1) * width] = (
            g / (1.0 + jnp.exp(-g)) * u * gate
        ).astype(jnp.bfloat16)


def up_call(place, tok, head, tail, mine, other):
    local, _, cols = mine[0].shape
    tokens = sum(v.shape[0] for v in head)
    lanes = head[0].shape[1] + tail[0].shape[1]
    count = len(head) + len(tail) + len(mine) + len(other)
    return pl.pallas_call(
        functools.partial(up_kernel, len(mine) // QUAD, len(head), len(tail), tok),
        in_specs=[pl.BlockSpec(memory_space=pltpu.SMEM)]
        + [pl.BlockSpec(memory_space=pltpu.VMEM)] * count,
        out_specs=pl.BlockSpec(memory_space=pltpu.VMEM),
        scratch_shapes=[pltpu.VMEM((tokens, lanes), jnp.bfloat16)],
        out_shape=jax.ShapeDtypeStruct((tokens, local * cols), jnp.bfloat16),
        compiler_params=pltpu.CompilerParams(vmem_limit_bytes=48 * 1024 * 1024),
        cost_estimate=pl.CostEstimate(flops=1, bytes_accessed=1, transcendentals=0),
        name="up",
    )(place, *head, *tail, *mine, *other)


def down_kernel(start, place_ref, h_ref, near_ref, near_other_ref, far_ref, far_other_ref, *out_refs):
    first = place_ref[0] == 0
    feats = near_ref.shape[1]
    order = [[], []]
    for e in range(near_ref.shape[0]):
        for near, far in ((near_ref[e], far_ref[e]), (near_other_ref[e], far_other_ref[e])):
            order[0].append(jnp.where(first, near, far))
            order[1].append(jnp.where(first, far, near))
    for j in range(2):
        partial = lax.dot_general(
            h_ref[start : start + out_refs[0].shape[0], :],
            jnp.concatenate(order[j], axis=1),
            (((1,), (1,)), ((), ())),
            preferred_element_type=jnp.float32,
        )
        if len(out_refs) == 2:
            out_refs[j][...] = partial.astype(out_refs[j].dtype)
        else:
            out_refs[0][:, j * feats : (j + 1) * feats] = partial.astype(out_refs[0].dtype)


def down_call(place, hidden, near, far, send, parts):
    tokens = hidden.shape[0] // 2
    feats = 2 * near[0].shape[1] // parts
    kind = jnp.bfloat16 if send else jnp.float32
    out = [jax.ShapeDtypeStruct((tokens, feats), kind)] * parts
    return pl.pallas_call(
        functools.partial(down_kernel, tokens if send else 0),
        in_specs=[pl.BlockSpec(memory_space=pltpu.SMEM)]
        + [pl.BlockSpec(memory_space=pltpu.VMEM)] * 5,
        out_specs=[pl.BlockSpec(memory_space=pltpu.VMEM)] * parts,
        out_shape=out,
        compiler_params=pltpu.CompilerParams(vmem_limit_bytes=40 * 1024 * 1024),
        cost_estimate=pl.CostEstimate(flops=1, bytes_accessed=1, transcendentals=0),
        name="down",
    )(place, hidden, *near, *far)


def body(
    attended,
    residual,
    out_weight,
    norm_gain,
    final_gain,
    routes,
    gate_logits,
    placement,
    gate_up,
    down_weight,
):
    ranks = lax.axis_size("dp")
    zones = lax.axis_size("expert")
    rows = ranks // QUAD
    me = lax.axis_index("dp")
    zone = lax.axis_index("expert")
    core, side, row = me % 2, (me // 2) % 2, me // QUAD
    tok, width = attended.shape
    local, depth, _ = gate_up.shape
    hid = down_weight.shape[2]
    part = hid // QUAD

    def flip(values, bit):
        return lax.ppermute(values, "dp", [(i, i ^ bit) for i in range(ranks)])

    def hop(values, bit):
        return lax.ppermute(values, "expert", [(i, i ^ bit) for i in range(zones)])

    def widen(pieces):
        bit = 1
        while bit < rows:
            pieces = pieces + [flip(p, bit * QUAD) for p in pieces]
            bit *= 2
        return pieces

    zone_bits = []
    while 1 << len(zone_bits) < zones:
        zone_bits.insert(0, 1 << len(zone_bits))

    place = jnp.stack([side, core, zone, jnp.int32(local), row]).astype(jnp.int32)

    gu_own, gu_away, gu_to_mate, gu_to_mate_away = cut_call(place, gate_up, part)
    stored, head, tail = front_call(
        place, rows, after(attended, gu_own), residual, out_weight, norm_gain, routes, gate_logits, placement
    )
    stream_in = stored.astype(jnp.float32)
    gu_own_x = flip(gu_away, 2)
    first = widen([gu_own])
    gu_mate, gu_mate_away = flip(gu_to_mate, 1), flip(gu_to_mate_away, 1)
    gu_mate_x = flip(gu_mate_away, 2)
    near = after(head, gu_mate, gu_mate_away)
    second = widen([after(gu_mate, head)])
    hops = []
    for bit in zone_bits[:-1]:
        hops.append(hop(near, bit))
        near = jnp.concatenate([near, hops[-1]], axis=0)
    gu_own_x, *first[1:] = after_all([gu_own_x, *first[1:]], hops[0])
    third = widen([gu_own_x])
    fourth = widen([after(gu_mate_x, second[-1])])
    mine = [p for group in zip(first, second, third, fourth) for p in group]
    shared = [flip(gu_own, 1), flip(gu_own_x, 1), flip(gu_mate_x, 1)]
    firsts, seconds, thirds, fourths = (
        [flip(p, 1) for p in group[1:]] for group in (first, second, third, fourth)
    )
    other = [gu_to_mate, shared[0], shared[2], shared[1]]
    for group in zip(seconds, firsts, fourths, thirds):
        other += group

    dn_own, dn_away, dn_to_mate, dn_to_mate_away = cut_call(
        place, after(down_weight, first[-1]), part
    )
    dn_mate, dn_mate_away = flip(dn_to_mate, 1), flip(dn_to_mate_away, 1)

    def pair(own, mate):
        return jnp.where(
            core == 0,
            jnp.concatenate([own, mate], axis=1),
            jnp.concatenate([mate, own], axis=1),
        )

    dn_near = pair(dn_own, dn_mate)
    dn_away = pair(dn_away, dn_mate_away)

    both = jnp.concatenate([tail, flip(tail, 2)], axis=0)
    for bit in zone_bits[:-1]:
        received = hop(after(both, hops[0]), bit)
        both = jnp.concatenate([both, received], axis=0)
    both_far = hop(both, zone_bits[-1])

    far = hop(after(near, second[-1], gu_mate_x), zone_bits[-1])
    near_x = flip(after(near, second[-1], received, shared[0], shared[1], *firsts), 2)
    far_x = flip(after(far, near_x, third[-1], dn_near, dn_away, shared[2], *seconds), 2)

    dn_far = flip(after(dn_away, far_x, *thirds), 2)

    hidden = up_call(place, tok, [near, far, near_x, far_x], [both, both_far], mine, other)
    dn_nears = widen([after(dn_near, third[-1])])
    hidden = after(hidden, dn_nears[-1])
    dn_fars = widen([after(dn_far, fourth[-1])])
    dn_nears = [(v, flip(after(v, hidden), 1)) for v in dn_nears]
    dn_fars = [(v, flip(after(v, hidden), 1)) for v in dn_fars]

    chunks, crossed = [], None
    for m in range(rows):
        parts = 2 if m == rows - 1 else 1
        ready = hidden if crossed is None else after(hidden, crossed)
        sends = down_call(place, ready, dn_nears[m], dn_fars[m], True, parts)
        keeps = down_call(place, after(hidden, sends[0]), dn_nears[m], dn_fars[m], False, parts)
        for send, keep in zip(sends, keeps):
            crossed = flip(send, 2)
            total = keep + crossed.astype(jnp.float32)
            for bit in reversed(zone_bits):
                size = total.shape[0] // 2
                moved = total[size:].astype(jnp.bfloat16)
                total = total[:size] + hop(moved, bit).astype(jnp.float32)
            chunks.append(total)
    branch = swap_blocks(jnp.concatenate(chunks, axis=1), row, rows)
    total = stream_in + branch
    return (total.astype(jnp.bfloat16), normalize(total, final_gain).astype(jnp.bfloat16))


def solution(mesh):
    tokens = P(("dp", "expert"), None)
    weights = P("expert", "dp", None)
    return jax.shard_map(
        body,
        mesh=mesh,
        in_specs=(tokens, tokens, P(), P(), P(), tokens, tokens, P(), weights, weights),
        out_specs=(tokens, tokens),
        check_vma=False,
    )
```

```python
import functools

import jax
import jax.numpy as jnp
from jax import lax
from jax.experimental import pallas as pl
from jax.experimental.pallas import tpu as pltpu
from jax.sharding import PartitionSpec as P

EPS = 1e-06
LOGIT_SCALE = 0.5
LANES = 128
LOW = 64
QUAD = 4


def normalize(values, gain):
    return values * lax.rsqrt(jnp.mean(values * values, axis=-1, keepdims=True) + EPS) * gain


def after(values, *others):
    return lax.optimization_barrier((values, *others))[0]


def after_all(values, *others):
    return lax.optimization_barrier((*values, *others))[: len(values)]


def swap_blocks(values, index, blocks):
    size = values.shape[1] // blocks
    bit = 1
    while bit < blocks:
        swapped = jnp.concatenate(
            [values[:, (m ^ bit) * size : ((m ^ bit) + 1) * size] for m in range(blocks)], axis=1
        )
        values = jnp.where((index & bit) != 0, swapped, values)
        bit *= 2
    return values


def swap_lanes(values, index, blocks):
    width = values.shape[1]
    size = width // blocks
    lane = lax.broadcasted_iota(jnp.int32, values.shape, 1)
    bit = 1
    while bit < blocks:
        step = bit * size
        upper = (lane // step) % 2 == 1
        swapped = jnp.where(
            upper, pltpu.roll(values, step, 1), pltpu.roll(values, width - step, 1)
        )
        values = jnp.where((index & bit) != 0, swapped, values)
        bit *= 2
    return values


def cut(part, side, core, weight, outs):
    blocks = outs[0].shape[2] // part
    targets = [(core, side), (core, 1 - side), (1 - core, side), (1 - core, 1 - side)]
    for out_ref, (c, s) in zip(outs, targets):
        for b in range(blocks):
            at = pl.multiple_of(b * QUAD * part + (2 * c + s) * part, part)
            out_ref[:, :, b * part : (b + 1) * part] = weight[:, :, pl.ds(at, part)]


def front_kernel(
    ranks,
    part,
    place_ref,
    att_ref,
    res_ref,
    gain_ref,
    routes_ref,
    logits_ref,
    placed_ref,
    w_hbm,
    gu_hbm,
    stream_ref,
    sent_ref,
    own_ref,
    away_ref,
    mate_ref,
    mate_away_ref,
    w_ref,
    gu_ref,
    keep_ref,
    sems,
):
    steps = w_ref.shape[0]
    width, cols = w_ref.shape[1:]
    load = pltpu.make_async_copy(gu_hbm, gu_ref, sems.at[steps])
    load.start()
    loads = []
    for i in range(steps):
        loads.append(
            pltpu.make_async_copy(w_hbm.at[:, i * cols : (i + 1) * cols], w_ref.at[i], sems.at[i])
        )
        loads[-1].start()

    load.wait()
    cut(part, place_ref[0], place_ref[1], gu_ref, (own_ref, away_ref, mate_ref, mate_away_ref))

    for i in range(steps):
        some = slice(i * cols, (i + 1) * cols)
        loads[i].wait()
        mixed = res_ref[:, some].astype(jnp.float32) + jnp.dot(
            att_ref[...], w_ref[i], preferred_element_type=jnp.float32
        )
        stored = mixed.astype(jnp.bfloat16)
        stream_ref[:, some] = stored
        keep_ref[:, some] = stored.astype(jnp.float32)

    normed = normalize(keep_ref[...], gain_ref[...])
    sent_ref[:, :width] = swap_lanes(normed, place_ref[3], ranks).astype(jnp.bfloat16)
    scores = jnp.exp(logits_ref[...].astype(jnp.float32) * LOGIT_SCALE)
    gates = scores / jnp.sum(scores, axis=1, keepdims=True)
    routes = routes_ref[...]
    spread = jnp.zeros((gates.shape[0], LANES), jnp.float32)
    for k in range(gates.shape[1]):
        hit = routes[:, k : k + 1] == placed_ref[...]
        spread = jnp.where(hit, gates[:, k : k + 1], spread)
    high = spread.astype(jnp.bfloat16).astype(jnp.float32)
    lane = lax.broadcasted_iota(jnp.int32, spread.shape, 1)
    sent_ref[:, width:] = jnp.where(lane < LOW, high, spread - high).astype(jnp.bfloat16)


def front_call(
    place, ranks, part, attended, residual, weight, gain, routes, logits, placement, gate_up
):
    tok, width = attended.shape
    local, depth, cols = gate_up.shape
    steps = 4
    padded = jnp.pad(placement, (0, LOW - placement.shape[0]), constant_values=-1)
    placed = jnp.concatenate([padded, padded])[None, :]
    vmem = pl.BlockSpec(memory_space=pltpu.VMEM)
    hbm = pl.BlockSpec(memory_space=pl.ANY)
    return pl.pallas_call(
        functools.partial(front_kernel, ranks, part),
        in_specs=[pl.BlockSpec(memory_space=pltpu.SMEM)] + [vmem] * 6 + [hbm] * 2,
        out_specs=[vmem] * 6,
        out_shape=[
            jax.ShapeDtypeStruct((tok, width), jnp.bfloat16),
            jax.ShapeDtypeStruct((tok, width + LANES), jnp.bfloat16),
        ]
        + [jax.ShapeDtypeStruct((local, depth, cols // QUAD), jnp.bfloat16)] * QUAD,
        scratch_shapes=[
            pltpu.VMEM((steps, width, width // steps), jnp.bfloat16),
            pltpu.VMEM(gate_up.shape, jnp.bfloat16),
            pltpu.VMEM((tok, width), jnp.float32),
            pltpu.SemaphoreType.DMA((steps + 1,)),
        ],
        compiler_params=pltpu.CompilerParams(vmem_limit_bytes=48 * 1024 * 1024),
        cost_estimate=pl.CostEstimate(flops=1, bytes_accessed=1, transcendentals=0),
        name="front",
    )(place, attended, residual, gain[None, :], routes, logits, placed, weight, gate_up)


def cut_kernel(part, place_ref, w_ref, *out_refs):
    cut(part, place_ref[0], place_ref[1], w_ref, out_refs)


def cut_call(place, weight, part):
    local, depth, cols = weight.shape
    out = jax.ShapeDtypeStruct((local, depth, cols // QUAD), jnp.bfloat16)
    return pl.pallas_call(
        functools.partial(cut_kernel, part),
        in_specs=[pl.BlockSpec(memory_space=pltpu.SMEM), pl.BlockSpec(memory_space=pltpu.VMEM)],
        out_specs=[pl.BlockSpec(memory_space=pltpu.VMEM)] * QUAD,
        out_shape=[out] * QUAD,
        compiler_params=pltpu.CompilerParams(vmem_limit_bytes=24 * 1024 * 1024),
        cost_estimate=pl.CostEstimate(flops=1, bytes_accessed=1, transcendentals=0),
        name="cut",
    )(place, weight)


def up_kernel(rows, count, place_ref, *refs):
    here, away = refs[:count], refs[count : 2 * count]
    pieces = refs[2 * count : 2 * count + 2 * QUAD * rows]
    out_ref, x_ref = refs[2 * count + 2 * QUAD * rows :]
    zone = place_ref[2]
    local, _, width = pieces[0].shape
    part = width // 2
    tok = here[0].shape[0]
    feats = x_ref.shape[1] - LANES
    half = feats // (2 * rows)

    for i in range(count):
        x_ref[i * tok : (i + 1) * tok, :] = here[i][...]
        some = slice((count + i) * tok, (count + i + 1) * tok)
        for j in range(2 * rows):
            to, come = j * half, (j ^ 1) * half
            x_ref[some, to : to + half] = away[i][:, come : come + half]
        x_ref[some, feats:] = away[i][:, feats:]

    lane = lax.broadcasted_iota(jnp.int32, (LANES, width), 0)
    for e in range(local):
        mine, other = (
            jnp.concatenate([p[e] for p in pieces[i * QUAD * rows : (i + 1) * QUAD * rows]], axis=0)
            for i in range(2)
        )
        w = jnp.concatenate(
            [mine[:, :part], other[:, :part], mine[:, part:], other[:, part:]], axis=1
        )
        slot = zone * local + e
        pick = jnp.where((lane == slot) | (lane == slot + LOW), 0.5, 0.0).astype(jnp.bfloat16)
        acc = jnp.dot(x_ref[:, :feats], w, preferred_element_type=jnp.float32)
        gate = jnp.dot(x_ref[:, feats:], pick, preferred_element_type=jnp.float32)
        g, u = acc[:, :width], acc[:, width:]
        out_ref[:, e * width : (e + 1) * width] = (
            (g + g * jnp.tanh(0.5 * g)) * (u * gate)
        ).astype(jnp.bfloat16)


def up_call(place, here, away, mine, other):
    local, _, cols = mine[0].shape
    tok, lanes = here[0].shape
    tokens = 2 * len(here) * tok
    operands = [*here, *away, *mine, *other]
    return pl.pallas_call(
        functools.partial(up_kernel, len(mine) // QUAD, len(here)),
        in_specs=[pl.BlockSpec(memory_space=pltpu.SMEM)]
        + [pl.BlockSpec(memory_space=pltpu.VMEM)] * len(operands),
        out_specs=pl.BlockSpec(memory_space=pltpu.VMEM),
        scratch_shapes=[pltpu.VMEM((tokens, lanes), jnp.bfloat16)],
        out_shape=jax.ShapeDtypeStruct((tokens, local * cols), jnp.bfloat16),
        compiler_params=pltpu.CompilerParams(vmem_limit_bytes=48 * 1024 * 1024),
        cost_estimate=pl.CostEstimate(flops=1, bytes_accessed=1, transcendentals=0),
        name="up",
    )(place, *operands)


def product(hidden, mine, other):
    w = [part[e] for e in range(mine.shape[0]) for part in (mine, other)]
    return lax.dot_general(
        hidden,
        jnp.concatenate(w, axis=1),
        (((1,), (1,)), ((), ())),
        preferred_element_type=jnp.float32,
    )


def down_kernel(start, h_ref, near_ref, near_other_ref, far_ref, far_other_ref, *out_refs):
    rows = out_refs[0].shape[0]
    feats = near_ref.shape[1]
    hidden = h_ref[start : start + rows, :]
    for j, pair in enumerate(((near_ref, near_other_ref), (far_ref, far_other_ref))):
        partial = product(hidden, *pair)
        if len(out_refs) == 2:
            out_refs[j][...] = partial.astype(out_refs[j].dtype)
        else:
            out_refs[0][:, j * feats : (j + 1) * feats] = partial.astype(out_refs[0].dtype)


def down_call(hidden, near, far, send, parts):
    tokens = hidden.shape[0] // 2
    feats = 2 * near[0].shape[1] // parts
    kind = jnp.bfloat16 if send else jnp.float32
    out = [jax.ShapeDtypeStruct((tokens, feats), kind)] * parts
    return pl.pallas_call(
        functools.partial(down_kernel, tokens if send else 0),
        in_specs=[pl.BlockSpec(memory_space=pltpu.VMEM)] * 5,
        out_specs=[pl.BlockSpec(memory_space=pltpu.VMEM)] * parts,
        out_shape=out,
        compiler_params=pltpu.CompilerParams(vmem_limit_bytes=40 * 1024 * 1024),
        cost_estimate=pl.CostEstimate(flops=1, bytes_accessed=1, transcendentals=0),
        name="down",
    )(hidden, *near, *far)


def body(
    attended,
    residual,
    out_weight,
    norm_gain,
    final_gain,
    routes,
    gate_logits,
    placement,
    gate_up,
    down_weight,
):
    ranks = lax.axis_size("dp")
    zones = lax.axis_size("expert")
    rows = ranks // QUAD
    me = lax.axis_index("dp")
    zone = lax.axis_index("expert")
    core, side = me % 2, (me // 2) % 2
    hid = down_weight.shape[2]
    part = hid // QUAD

    def flip(values, bit):
        return lax.ppermute(values, "dp", [(i, i ^ bit) for i in range(ranks)])

    def hop(values, bit):
        return lax.ppermute(values, "expert", [(i, i ^ bit) for i in range(zones)])

    def widen(pieces):
        bit = 1
        while bit < rows:
            pieces = pieces + [flip(p, bit * QUAD) for p in pieces]
            bit *= 2
        return pieces

    zone_bits = []
    while 1 << len(zone_bits) < zones:
        zone_bits.append(1 << len(zone_bits))
    place = jnp.stack([side, core, zone, me]).astype(jnp.int32)

    stored, sent, gu_own, gu_away, gu_to_mate, gu_to_mate_away = front_call(
        place,
        ranks,
        part,
        attended,
        residual,
        out_weight,
        norm_gain,
        routes,
        gate_logits,
        placement,
        gate_up,
    )
    stream_in = stored.astype(jnp.float32)
    gu_own_x = flip(gu_away, 2)
    first = widen([gu_own])
    gu_mate, gu_mate_away = flip(gu_to_mate, 1), flip(gu_to_mate_away, 1)
    near = [sent]
    for bit in reversed(zone_bits[1:]):
        near = near + [hop(v, bit) for v in near]
    gu_own, gu_own_x, gu_mate, gu_mate_away, *both = after_all(
        [gu_own, gu_own_x, gu_mate, gu_mate_away, *first[1:], *near]
    )
    first, near = [gu_own, *both[: rows - 1]], both[rows - 1 :]
    gu_mate_x = flip(gu_mate_away, 2)
    second = widen([gu_mate])
    far = [hop(v, 1) for v in near]
    shared = [flip(gu_own, 1), flip(gu_own_x, 1)]
    firsts = [flip(p, 1) for p in first[1:]]
    gu_own_x, gu_mate, gu_mate_x, *both = after_all(
        [gu_own_x, gu_mate, gu_mate_x, *second[1:], *near, *far], *shared, *firsts
    )
    second, near, far = (
        [gu_mate, *both[: rows - 1]],
        both[rows - 1 : rows - 1 + len(near)],
        both[rows - 1 + len(near) :],
    )
    near_x = [flip(v, 2) for v in near]
    third = widen([gu_own_x])
    shared.append(flip(gu_mate_x, 1))
    seconds = [flip(p, 1) for p in second[1:]]
    gu_own_x, gu_mate_x, *both = after_all(
        [gu_own_x, gu_mate_x, *third[1:], *near_x, *far], shared[-1], *seconds
    )
    third, near_x, far = (
        [gu_own_x, *both[: rows - 1]],
        both[rows - 1 : rows - 1 + len(near)],
        both[rows - 1 + len(near) :],
    )
    far_x = [flip(v, 2) for v in far]
    fourth = widen([gu_mate_x])
    thirds = [flip(p, 1) for p in third[1:]]
    fourths = [flip(p, 1) for p in fourth[1:]]
    here, away = near + far, near_x + far_x
    mine = [p for group in zip(first, second, third, fourth) for p in group]
    other = [gu_to_mate, shared[0], shared[2], shared[1]]
    for group in zip(seconds, firsts, fourths, thirds):
        other += group

    dn_own, dn_away, dn_to_mate, dn_to_mate_away = cut_call(
        place, after(down_weight, first[-1]), part
    )
    dn_mate, dn_mate_away = flip(dn_to_mate, 1), flip(dn_to_mate_away, 1)

    def pair(own, mate):
        return jnp.where(
            core == 0,
            jnp.concatenate([own, mate], axis=1),
            jnp.concatenate([mate, own], axis=1),
        )

    dn_near, dn_away = pair(dn_own, dn_mate), pair(dn_away, dn_mate_away)
    dn_near_other = flip(dn_near, 1)

    dn_far = flip(after(dn_away, *far_x, fourth[-1], dn_near_other, *thirds), 2)
    hidden = up_call(place, here, away, mine, other)
    dn_nears = widen([after(dn_near, *far_x, fourth[-1])])
    hidden = after(hidden, dn_nears[-1])
    dn_fars = widen([after(dn_far, fourth[-1])])
    nears = [(dn_near, dn_near_other)] + [(v, flip(after(v, hidden), 1)) for v in dn_nears[1:]]
    fars = [(v, flip(after(v, hidden), 1)) for v in dn_fars]

    chunks, crossed = [], None
    for m in range(rows):
        parts = 2 if m == rows - 1 else 1
        ready = hidden if crossed is None else after(hidden, crossed)
        sends = down_call(ready, nears[m], fars[m], True, parts)
        keeps = down_call(after(hidden, sends[0]), nears[m], fars[m], False, parts)
        for i, keep in enumerate(keeps):
            crossed = flip(sends[parts - 1 - i], 2)
            if parts == 1:
                size = crossed.shape[1] // 2
                total = keep + jnp.concatenate(
                    [crossed[:, size:], crossed[:, :size]], axis=1
                ).astype(jnp.float32)
            else:
                total = keep + crossed.astype(jnp.float32)
            for bit in zone_bits:
                size = total.shape[0] // 2
                moved = total[size:].astype(jnp.bfloat16)
                total = total[:size] + hop(moved, bit).astype(jnp.float32)
            chunks.append(total)
    branch = swap_blocks(jnp.concatenate(chunks, axis=1), me // 2, 2 * rows)
    total = stream_in + branch
    return (total.astype(jnp.bfloat16), normalize(total, final_gain).astype(jnp.bfloat16))


def solution(mesh):
    tokens = P(("dp", "expert"), None)
    weights = P("expert", "dp", None)
    return jax.shard_map(
        body,
        mesh=mesh,
        in_specs=(tokens, tokens, P(), P(), P(), tokens, tokens, P(), weights, weights),
        out_specs=(tokens, tokens),
        check_vma=False,
    )
```

```python
import functools

import jax
import jax.numpy as jnp
from jax import lax
from jax.experimental import pallas as pl
from jax.experimental.pallas import tpu as pltpu
from jax.sharding import PartitionSpec as P

EPS = 1e-06
LOGIT_SCALE = 0.5
LANES = 128
LOW = 64
QUAD = 4


def normalize(values, gain):
    return values * lax.rsqrt(jnp.mean(values * values, axis=-1, keepdims=True) + EPS) * gain


def after(values, *others):
    return lax.optimization_barrier((values, *others))[0]


def after_all(values, *others):
    return list(lax.optimization_barrier((*values, *others)))[: len(values)]


def swap_blocks(values, index, blocks):
    size = values.shape[1] // blocks
    bit = 1
    while bit < blocks:
        swapped = jnp.concatenate(
            [values[:, (m ^ bit) * size : ((m ^ bit) + 1) * size] for m in range(blocks)], axis=1
        )
        values = jnp.where((index & bit) != 0, swapped, values)
        bit *= 2
    return values


def swap_lanes(values, index, blocks):
    width = values.shape[1]
    size = width // blocks
    lane = lax.broadcasted_iota(jnp.int32, values.shape, 1)
    bit = 1
    while bit < blocks:
        step = bit * size
        upper = (lane // step) % 2 == 1
        swapped = jnp.where(
            upper, pltpu.roll(values, step, 1), pltpu.roll(values, width - step, 1)
        )
        values = jnp.where((index & bit) != 0, swapped, values)
        bit *= 2
    return values


def front_kernel(
    ranks,
    att_ref,
    res_ref,
    w_ref,
    gain_ref,
    routes_ref,
    logits_ref,
    placed_ref,
    stream_ref,
    sent_ref,
    keep_ref,
):
    step = pl.program_id(0)
    cols = w_ref.shape[1]
    width = att_ref.shape[1]
    mixed = res_ref[...].astype(jnp.float32) + jnp.dot(
        att_ref[...], w_ref[...], preferred_element_type=jnp.float32
    )
    stored = mixed.astype(jnp.bfloat16)
    stream_ref[...] = stored
    keep_ref[:, pl.ds(pl.multiple_of(step * cols, cols), cols)] = stored.astype(jnp.float32)

    @pl.when(step == pl.num_programs(0) - 1)
    def _():
        normed = normalize(keep_ref[...], gain_ref[...])
        sent_ref[:, :width] = swap_lanes(normed, lax.axis_index("dp") // 2, ranks // 2).astype(jnp.bfloat16)
        scores = jnp.exp(logits_ref[...].astype(jnp.float32) * LOGIT_SCALE)
        gates = scores / jnp.sum(scores, axis=1, keepdims=True)
        routes = routes_ref[...]
        spread = jnp.zeros((gates.shape[0], LANES), jnp.float32)
        for k in range(gates.shape[1]):
            hit = routes[:, k : k + 1] == placed_ref[...]
            spread = jnp.where(hit, gates[:, k : k + 1], spread)
        high = spread.astype(jnp.bfloat16).astype(jnp.float32)
        lane = lax.broadcasted_iota(jnp.int32, spread.shape, 1)
        sent_ref[:, width:] = jnp.where(lane < LOW, high, spread - high).astype(jnp.bfloat16)


def front_call(ranks, attended, residual, weight, gain, routes, logits, placement):
    tok, width = attended.shape
    steps = 4
    cols = width // steps
    padded = jnp.pad(placement, (0, LOW - placement.shape[0]), constant_values=-1)
    placed = jnp.concatenate([padded, padded])[None, :]
    whole = lambda shape: pl.BlockSpec(shape, lambda i: (0, 0))
    return pl.pallas_call(
        functools.partial(front_kernel, ranks),
        grid=(steps,),
        in_specs=[
            whole((tok, width)),
            pl.BlockSpec((tok, cols), lambda i: (0, i)),
            pl.BlockSpec((width, cols), lambda i: (0, i)),
            whole((1, width)),
            whole(routes.shape),
            whole(logits.shape),
            whole((1, LANES)),
        ],
        out_specs=[
            pl.BlockSpec((tok, cols), lambda i: (0, i)),
            whole((tok, width + LANES)),
        ],
        out_shape=[
            jax.ShapeDtypeStruct((tok, width), jnp.bfloat16),
            jax.ShapeDtypeStruct((tok, width + LANES), jnp.bfloat16),
        ],
        scratch_shapes=[pltpu.VMEM((tok, width), jnp.float32)],
        compiler_params=pltpu.CompilerParams(vmem_limit_bytes=12 * 1024 * 1024),
        cost_estimate=pl.CostEstimate(flops=1, bytes_accessed=1, transcendentals=0),
        name="front",
    )(attended, residual, weight, gain[None, :], routes, logits, placed)


def cut(weight, out_ref, rows, part, c, s):
    for b in range(out_ref.shape[2] // part):
        at = pl.multiple_of(b * QUAD * part + (2 * c + s) * part, part)
        out_ref[:, rows, b * part : (b + 1) * part] = weight[:, :, pl.ds(at, part)]


def give_kernel(part, w_ref, near_ref, away_ref):
    core, side = lax.axis_index("dp") % 2, (lax.axis_index("dp") // 2) % 2
    cut(w_ref, near_ref, slice(None), part, 1 - core, side)
    cut(w_ref, away_ref, slice(None), part, 1 - core, 1 - side)


def join_kernel(part, w_ref, near_in_ref, away_in_ref, near_ref, away_ref):
    core, side = lax.axis_index("dp") % 2, (lax.axis_index("dp") // 2) % 2
    depth = w_ref.shape[1]
    here = pl.ds(pl.multiple_of(core * depth, depth), depth)
    there = pl.ds(pl.multiple_of((1 - core) * depth, depth), depth)
    cut(w_ref, near_ref, here, part, core, side)
    cut(w_ref, away_ref, here, part, core, 1 - side)
    near_ref[:, there, :] = near_in_ref[...]
    away_ref[:, there, :] = away_in_ref[...]


def weight_call(kernel, name, depth, part, weight, *received):
    local, _, cols = weight.shape
    out = jax.ShapeDtypeStruct((local, depth, cols // QUAD), jnp.bfloat16)
    whole = lambda v: pl.BlockSpec(v.shape, lambda i: (0, 0, 0))
    return pl.pallas_call(
        functools.partial(kernel, part),
        grid=(1,),
        in_specs=[whole(v) for v in (weight, *received)],
        out_specs=[whole(out)] * 2,
        out_shape=[out] * 2,
        compiler_params=pltpu.CompilerParams(vmem_limit_bytes=16 * 1024 * 1024),
        cost_estimate=pl.CostEstimate(flops=1, bytes_accessed=1, transcendentals=0),
        name=name,
    )(weight, *received)


def up_kernel(rows, count, *refs):
    here, away = refs[:count], refs[count : 2 * count]
    pieces = refs[2 * count : 2 * count + 4 * rows]
    out_ref, x_ref = refs[2 * count + 4 * rows :]
    zone = lax.axis_index("expert")
    local, half, width = pieces[0].shape
    part = width // 2
    feats = x_ref.shape[1] - LANES
    middle = x_ref.shape[0] // 2

    at = 0
    for block, across in zip(here, away):
        some = slice(at, at + block.shape[0])
        x_ref[some, :] = block[...]
        some = slice(middle + at, middle + at + block.shape[0])
        for j in range(2 * rows):
            to, come = j * half, (j ^ 1) * half
            x_ref[some, to : to + half] = across[:, come : come + half]
        x_ref[some, feats:] = across[:, feats:]
        at += block.shape[0]

    lane = lax.broadcasted_iota(jnp.int32, (LANES, width), 0)
    for e in range(local):
        mine, other = (
            jnp.concatenate([p[e] for p in pieces[2 * i * rows : 2 * (i + 1) * rows]], axis=0)
            for i in range(2)
        )
        w = jnp.concatenate(
            [mine[:, :part], other[:, :part], mine[:, part:], other[:, part:]], axis=1
        )
        slot = zone * local + e
        pick = jnp.where((lane == slot) | (lane == slot + LOW), 0.5, 0.0).astype(jnp.bfloat16)
        acc = jnp.dot(x_ref[:, :feats], w, preferred_element_type=jnp.float32)
        gate = jnp.dot(x_ref[:, feats:], pick, preferred_element_type=jnp.float32)
        g, u = acc[:, :width], acc[:, width:]
        out_ref[:, e * width : (e + 1) * width] = (
            (g + g * jnp.tanh(0.5 * g)) * (u * gate)
        ).astype(jnp.bfloat16)


def up_call(here, away, mine, other):
    local, _, cols = mine[0].shape
    lanes = here[0].shape[1]
    tokens = 2 * sum(v.shape[0] for v in here)
    operands = [*here, *away, *mine, *other]
    return pl.pallas_call(
        functools.partial(up_kernel, len(mine) // 2, len(here)),
        in_specs=[pl.BlockSpec(memory_space=pltpu.VMEM)] * len(operands),
        out_specs=pl.BlockSpec(memory_space=pltpu.VMEM),
        scratch_shapes=[pltpu.VMEM((tokens, lanes), jnp.bfloat16)],
        out_shape=jax.ShapeDtypeStruct((tokens, local * cols), jnp.bfloat16),
        compiler_params=pltpu.CompilerParams(vmem_limit_bytes=28 * 1024 * 1024),
        cost_estimate=pl.CostEstimate(flops=1, bytes_accessed=1, transcendentals=0),
        name="up",
    )(*operands)


def product(hidden, mine, other):
    w = [part[e] for e in range(mine.shape[0]) for part in (mine, other)]
    return lax.dot_general(
        hidden,
        jnp.concatenate(w, axis=1),
        (((1,), (1,)), ((), ())),
        preferred_element_type=jnp.float32,
    )


def down_kernel(start, h_ref, near_ref, near_other_ref, far_ref, far_other_ref, *out_refs):
    rows = out_refs[0].shape[0]
    feats = near_ref.shape[1]
    hidden = h_ref[start : start + rows, :]
    for j, pair in enumerate(((near_ref, near_other_ref), (far_ref, far_other_ref))):
        partial = product(hidden, *pair)
        if len(out_refs) == 2:
            out_refs[j][...] = partial.astype(out_refs[j].dtype)
        else:
            out_refs[0][:, j * feats : (j + 1) * feats] = partial.astype(out_refs[0].dtype)


def down_call(hidden, near, far, send, parts):
    tokens = hidden.shape[0] // 2
    feats = 2 * near[0].shape[1] // parts
    kind = jnp.bfloat16 if send else jnp.float32
    out = [jax.ShapeDtypeStruct((tokens, feats), kind)] * parts
    return pl.pallas_call(
        functools.partial(down_kernel, tokens if send else 0),
        in_specs=[pl.BlockSpec(memory_space=pltpu.VMEM)] * 5,
        out_specs=[pl.BlockSpec(memory_space=pltpu.VMEM)] * parts,
        out_shape=out,
        compiler_params=pltpu.CompilerParams(vmem_limit_bytes=16 * 1024 * 1024),
        cost_estimate=pl.CostEstimate(flops=1, bytes_accessed=1, transcendentals=0),
        name="down",
    )(hidden, *near, *far)


def body(
    attended,
    residual,
    out_weight,
    norm_gain,
    final_gain,
    routes,
    gate_logits,
    placement,
    gate_up,
    down_weight,
):
    ranks = lax.axis_size("dp")
    zones = lax.axis_size("expert")
    rows = ranks // QUAD
    me = lax.axis_index("dp")
    hid = down_weight.shape[2]
    part = hid // QUAD

    def flip(values, bit):
        return lax.ppermute(values, "dp", [(i, i ^ bit) for i in range(ranks)])

    def hop(values, bit):
        return lax.ppermute(values, "expert", [(i, i ^ bit) for i in range(zones)])

    def widen(pieces):
        bit = 1
        while bit < rows:
            pieces = pieces + [flip(p, bit * QUAD) for p in pieces]
            bit *= 2
        return pieces

    zone_bits = []
    while 1 << len(zone_bits) < zones:
        zone_bits.append(1 << len(zone_bits))
    depth = gate_up.shape[1]
    give = weight_call(give_kernel, "give", depth, part, gate_up)
    got = [flip(v, 1) for v in give]
    gu_near, gu_away = weight_call(join_kernel, "join", 2 * depth, part, gate_up, *got)
    gu_far = flip(gu_away, 2)
    gu_nears = widen([gu_near])

    stored, sent = front_call(
        ranks,
        after(attended, give[0]),
        residual,
        out_weight,
        norm_gain,
        routes,
        gate_logits,
        placement,
    )
    stream_in = stored.astype(jnp.float32)
    near = sent
    for bit in reversed(zone_bits[1:]):
        near = jnp.concatenate([near, hop(near, bit)], axis=0)
    far = hop(near, 1)
    gu_near_other = flip(gu_near, 1)
    near_x = flip(after(near, gu_far, gu_near_other), 2)
    gu_fars = widen([after(gu_far, gu_nears[-1])])
    gu_nears_other = [gu_near_other] + [flip(v, 1) for v in gu_nears[1:]]
    gu_far_other = flip(gu_far, 1)
    far_x = flip(after(far, near_x, gu_far_other, *gu_nears_other[1:]), 2)
    gu_fars_other = [gu_far_other] + [flip(v, 1) for v in gu_fars[1:]]
    mine = [v for pair in zip(gu_nears, gu_fars) for v in pair]
    other = [v for pair in zip(gu_nears_other, gu_fars_other) for v in pair]

    down_weight = after(down_weight, sent)
    give = weight_call(give_kernel, "give", depth, part, down_weight)
    got = [flip(v, 1) for v in give]
    dn_near, dn_away = weight_call(join_kernel, "join", 2 * depth, part, down_weight, *got)
    dn_near_other = flip(dn_near, 1)
    dn_far = flip(after(dn_away, far_x, dn_near_other), 2)
    dn_nears = widen([after(dn_near, gu_fars[-1])])

    hidden = up_call([near, far], [near_x, far_x], mine, other)
    hidden = after(hidden, dn_nears[-1])
    dn_far = after(dn_far, hidden)
    dn_fars = widen([dn_far])
    nears = [(dn_near, dn_near_other)] + [(v, flip(after(v, hidden), 1)) for v in dn_nears[1:]]
    fars = [(dn_far, flip(dn_far, 1))]

    chunks, crossed = [], []
    for m in range(rows):
        parts = 2 if m == rows - 1 else 1
        if m > 0:
            fars.append((dn_fars[m], flip(after(dn_fars[m], sends[0]), 1)))
        sends = down_call(after(hidden, *crossed), nears[m], fars[m], True, parts)
        keeps = down_call(after(hidden, sends[0]), nears[m], fars[m], False, parts)
        crossed = []
        for i, keep in enumerate(keeps):
            crossed.append(flip(sends[parts - 1 - i], 2))
            total = crossed[-1]
            if parts == 1:
                size = total.shape[1] // 2
                total = jnp.concatenate([total[:, size:], total[:, :size]], axis=1)
            total = keep + total.astype(jnp.float32)
            for bit in zone_bits:
                size = total.shape[0] // 2
                moved = total[size:].astype(jnp.bfloat16)
                total = total[:size] + hop(moved, bit).astype(jnp.float32)
            chunks.append(total)
    branch = swap_blocks(jnp.concatenate(chunks, axis=1), me // 2, 2 * rows)
    total = stream_in + branch
    return (total.astype(jnp.bfloat16), normalize(total, final_gain).astype(jnp.bfloat16))


def solution(mesh):
    tokens = P(("dp", "expert"), None)
    weights = P("expert", "dp", None)
    return jax.shard_map(
        body,
        mesh=mesh,
        in_specs=(tokens, tokens, P(), P(), P(), tokens, tokens, P(), weights, weights),
        out_specs=(tokens, tokens),
        check_vma=False,
    )
```

```python
import functools

import jax
import jax.numpy as jnp
from jax import lax
from jax.experimental import pallas as pl
from jax.experimental.pallas import tpu as pltpu
from jax.sharding import PartitionSpec as P

EPS = 1e-06
LOGIT_SCALE = 0.5
LANES = 128
LOW = 64
QUAD = 4


def normalize(values, gain):
    return values * lax.rsqrt(jnp.mean(values * values, axis=-1, keepdims=True) + EPS) * gain


def after(values, *others):
    return lax.optimization_barrier((values, *others))[0]


def after_all(values, *others):
    return list(lax.optimization_barrier((*values, *others)))[: len(values)]


def swap_blocks(values, index, blocks):
    size = values.shape[1] // blocks
    bit = 1
    while bit < blocks:
        swapped = jnp.concatenate(
            [values[:, (m ^ bit) * size : ((m ^ bit) + 1) * size] for m in range(blocks)], axis=1
        )
        values = jnp.where((index & bit) != 0, swapped, values)
        bit *= 2
    return values


def swap_lanes(values, index, blocks):
    width = values.shape[1]
    size = width // blocks
    lane = lax.broadcasted_iota(jnp.int32, values.shape, 1)
    bit = 1
    while bit < blocks:
        step = bit * size
        upper = (lane // step) % 2 == 1
        swapped = jnp.where(
            upper, pltpu.roll(values, step, 1), pltpu.roll(values, width - step, 1)
        )
        values = jnp.where((index & bit) != 0, swapped, values)
        bit *= 2
    return values


def front_kernel(
    ranks,
    att_ref,
    res_ref,
    w_ref,
    gain_ref,
    routes_ref,
    logits_ref,
    placed_ref,
    stream_ref,
    sent_ref,
    keep_ref,
):
    step = pl.program_id(0)
    cols = w_ref.shape[1]
    width = att_ref.shape[1]
    mixed = res_ref[...].astype(jnp.float32) + jnp.dot(
        att_ref[...], w_ref[...], preferred_element_type=jnp.float32
    )
    stored = mixed.astype(jnp.bfloat16)
    stream_ref[...] = stored
    keep_ref[:, pl.ds(pl.multiple_of(step * cols, cols), cols)] = stored.astype(jnp.float32)

    @pl.when(step == pl.num_programs(0) - 1)
    def _():
        normed = normalize(keep_ref[...], gain_ref[...])
        sent_ref[:, :width] = swap_lanes(normed, lax.axis_index("dp") // 2, ranks // 2).astype(jnp.bfloat16)
        scores = jnp.exp(logits_ref[...].astype(jnp.float32) * LOGIT_SCALE)
        gates = scores / jnp.sum(scores, axis=1, keepdims=True)
        routes = routes_ref[...]
        spread = jnp.zeros((gates.shape[0], LANES), jnp.float32)
        for k in range(gates.shape[1]):
            hit = routes[:, k : k + 1] == placed_ref[...]
            spread = jnp.where(hit, gates[:, k : k + 1], spread)
        high = spread.astype(jnp.bfloat16).astype(jnp.float32)
        lane = lax.broadcasted_iota(jnp.int32, spread.shape, 1)
        sent_ref[:, width:] = jnp.where(lane < LOW, high, spread - high).astype(jnp.bfloat16)


def front_call(ranks, attended, residual, weight, gain, routes, logits, placement):
    tok, width = attended.shape
    steps = 4
    cols = width // steps
    padded = jnp.pad(placement, (0, LOW - placement.shape[0]), constant_values=-1)
    placed = jnp.concatenate([padded, padded])[None, :]
    whole = lambda shape: pl.BlockSpec(shape, lambda i: (0, 0))
    return pl.pallas_call(
        functools.partial(front_kernel, ranks),
        grid=(steps,),
        in_specs=[
            whole((tok, width)),
            pl.BlockSpec((tok, cols), lambda i: (0, i)),
            pl.BlockSpec((width, cols), lambda i: (0, i)),
            whole((1, width)),
            whole(routes.shape),
            whole(logits.shape),
            whole((1, LANES)),
        ],
        out_specs=[
            pl.BlockSpec((tok, cols), lambda i: (0, i)),
            whole((tok, width + LANES)),
        ],
        out_shape=[
            jax.ShapeDtypeStruct((tok, width), jnp.bfloat16),
            jax.ShapeDtypeStruct((tok, width + LANES), jnp.bfloat16),
        ],
        scratch_shapes=[pltpu.VMEM((tok, width), jnp.float32)],
        compiler_params=pltpu.CompilerParams(vmem_limit_bytes=12 * 1024 * 1024),
        cost_estimate=pl.CostEstimate(flops=1, bytes_accessed=1, transcendentals=0),
        name="front",
    )(attended, residual, weight, gain[None, :], routes, logits, placed)


def cut(weight, out_ref, rows, part, c, s):
    for b in range(out_ref.shape[2] // part):
        at = pl.multiple_of(b * QUAD * part + (2 * c + s) * part, part)
        out_ref[:, rows, b * part : (b + 1) * part] = weight[:, :, pl.ds(at, part)]


def give_kernel(part, w_ref, near_ref, away_ref):
    core, side = lax.axis_index("dp") % 2, (lax.axis_index("dp") // 2) % 2
    cut(w_ref, near_ref, slice(None), part, 1 - core, side)
    cut(w_ref, away_ref, slice(None), part, 1 - core, 1 - side)


def join_kernel(part, w_ref, near_in_ref, away_in_ref, near_ref, away_ref):
    core, side = lax.axis_index("dp") % 2, (lax.axis_index("dp") // 2) % 2
    depth = w_ref.shape[1]
    here = pl.ds(pl.multiple_of(core * depth, depth), depth)
    there = pl.ds(pl.multiple_of((1 - core) * depth, depth), depth)
    cut(w_ref, near_ref, here, part, core, side)
    cut(w_ref, away_ref, here, part, core, 1 - side)
    near_ref[:, there, :] = near_in_ref[...]
    away_ref[:, there, :] = away_in_ref[...]


def weight_call(kernel, name, depth, part, weight, *received):
    local, _, cols = weight.shape
    out = jax.ShapeDtypeStruct((local, depth, cols // QUAD), jnp.bfloat16)
    whole = lambda v: pl.BlockSpec(v.shape, lambda i: (0, 0, 0))
    return pl.pallas_call(
        functools.partial(kernel, part),
        grid=(1,),
        in_specs=[whole(v) for v in (weight, *received)],
        out_specs=[whole(out)] * 2,
        out_shape=[out] * 2,
        compiler_params=pltpu.CompilerParams(vmem_limit_bytes=16 * 1024 * 1024),
        cost_estimate=pl.CostEstimate(flops=1, bytes_accessed=1, transcendentals=0),
        name=name,
    )(weight, *received)


def up_kernel(rows, count, *refs):
    here, away = refs[:count], refs[count : 2 * count]
    pieces = refs[2 * count : 2 * count + 4 * rows]
    out_ref, x_ref = refs[2 * count + 4 * rows :]
    zone = lax.axis_index("expert")
    local, half, width = pieces[0].shape
    part = width // 2
    feats = x_ref.shape[1] - LANES
    middle = x_ref.shape[0] // 2

    at = 0
    for block, across in zip(here, away):
        some = slice(at, at + block.shape[0])
        x_ref[some, :] = block[...]
        some = slice(middle + at, middle + at + block.shape[0])
        for j in range(2 * rows):
            to, come = j * half, (j ^ 1) * half
            x_ref[some, to : to + half] = across[:, come : come + half]
        x_ref[some, feats:] = across[:, feats:]
        at += block.shape[0]

    lane = lax.broadcasted_iota(jnp.int32, (LANES, width), 0)
    for e in range(local):
        mine, other = (
            jnp.concatenate([p[e] for p in pieces[2 * i * rows : 2 * (i + 1) * rows]], axis=0)
            for i in range(2)
        )
        w = jnp.concatenate(
            [mine[:, :part], other[:, :part], mine[:, part:], other[:, part:]], axis=1
        )
        slot = zone * local + e
        pick = jnp.where((lane == slot) | (lane == slot + LOW), 0.5, 0.0).astype(jnp.bfloat16)
        acc = jnp.dot(x_ref[:, :feats], w, preferred_element_type=jnp.float32)
        gate = jnp.dot(x_ref[:, feats:], pick, preferred_element_type=jnp.float32)
        g, u = acc[:, :width], acc[:, width:]
        out_ref[:, e * width : (e + 1) * width] = (
            (g + g * jnp.tanh(0.5 * g)) * (u * gate)
        ).astype(jnp.bfloat16)


def up_call(here, away, mine, other):
    local, _, cols = mine[0].shape
    lanes = here[0].shape[1]
    tokens = 2 * sum(v.shape[0] for v in here)
    operands = [*here, *away, *mine, *other]
    return pl.pallas_call(
        functools.partial(up_kernel, len(mine) // 2, len(here)),
        in_specs=[pl.BlockSpec(memory_space=pltpu.VMEM)] * len(operands),
        out_specs=pl.BlockSpec(memory_space=pltpu.VMEM),
        scratch_shapes=[pltpu.VMEM((tokens, lanes), jnp.bfloat16)],
        out_shape=jax.ShapeDtypeStruct((tokens, local * cols), jnp.bfloat16),
        compiler_params=pltpu.CompilerParams(vmem_limit_bytes=28 * 1024 * 1024),
        cost_estimate=pl.CostEstimate(flops=1, bytes_accessed=1, transcendentals=0),
        name="up",
    )(*operands)


def product(hidden, mine, other):
    w = [part[e] for e in range(mine.shape[0]) for part in (mine, other)]
    return lax.dot_general(
        hidden,
        jnp.concatenate(w, axis=1),
        (((1,), (1,)), ((), ())),
        preferred_element_type=jnp.float32,
    )


def down_kernel(start, h_ref, near_ref, near_other_ref, far_ref, far_other_ref, *out_refs):
    rows = out_refs[0].shape[0]
    feats = near_ref.shape[1]
    hidden = h_ref[start : start + rows, :]
    for j, pair in enumerate(((near_ref, near_other_ref), (far_ref, far_other_ref))):
        partial = product(hidden, *pair)
        if len(out_refs) == 2:
            out_refs[j][...] = partial.astype(out_refs[j].dtype)
        else:
            out_refs[0][:, j * feats : (j + 1) * feats] = partial.astype(out_refs[0].dtype)


def down_call(hidden, near, far, send, parts):
    tokens = hidden.shape[0] // 2
    feats = 2 * near[0].shape[1] // parts
    kind = jnp.bfloat16 if send else jnp.float32
    out = [jax.ShapeDtypeStruct((tokens, feats), kind)] * parts
    return pl.pallas_call(
        functools.partial(down_kernel, tokens if send else 0),
        in_specs=[pl.BlockSpec(memory_space=pltpu.VMEM)] * 5,
        out_specs=[pl.BlockSpec(memory_space=pltpu.VMEM)] * parts,
        out_shape=out,
        compiler_params=pltpu.CompilerParams(vmem_limit_bytes=16 * 1024 * 1024),
        cost_estimate=pl.CostEstimate(flops=1, bytes_accessed=1, transcendentals=0),
        name="down",
    )(hidden, *near, *far)


def body(
    attended,
    residual,
    out_weight,
    norm_gain,
    final_gain,
    routes,
    gate_logits,
    placement,
    gate_up,
    down_weight,
):
    ranks = lax.axis_size("dp")
    zones = lax.axis_size("expert")
    rows = ranks // QUAD
    me = lax.axis_index("dp")
    hid = down_weight.shape[2]
    part = hid // QUAD

    def flip(values, bit):
        return lax.ppermute(values, "dp", [(i, i ^ bit) for i in range(ranks)])

    def hop(values, bit):
        return lax.ppermute(values, "expert", [(i, i ^ bit) for i in range(zones)])

    def widen(pieces):
        bit = 1
        while bit < rows:
            pieces = pieces + [flip(p, bit * QUAD) for p in pieces]
            bit *= 2
        return pieces

    zone_bits = []
    while 1 << len(zone_bits) < zones:
        zone_bits.append(1 << len(zone_bits))
    depth = gate_up.shape[1]
    give = weight_call(give_kernel, "give", depth, part, gate_up)
    got = [flip(v, 1) for v in give]
    gu_near, gu_away = weight_call(join_kernel, "join", 2 * depth, part, gate_up, *got)
    gu_far = flip(gu_away, 2)
    gu_nears = widen([gu_near])

    stored, sent = front_call(
        ranks,
        after(attended, give[0]),
        residual,
        out_weight,
        norm_gain,
        routes,
        gate_logits,
        placement,
    )
    stream_in = stored.astype(jnp.float32)
    near = sent
    for bit in reversed(zone_bits[1:]):
        near = jnp.concatenate([near, hop(near, bit)], axis=0)
    far = hop(near, 1)
    gu_near_other = flip(gu_near, 1)
    near_x = flip(after(near, gu_near_other), 2)
    gu_fars = widen([after(gu_far, gu_nears[-1])])
    gu_nears_other = [gu_near_other] + [flip(v, 1) for v in gu_nears[1:]]
    gu_far_other = flip(gu_far, 1)
    far_x = flip(after(far, near_x, gu_far_other, *gu_nears_other[1:]), 2)
    gu_fars_other = [gu_far_other] + [flip(v, 1) for v in gu_fars[1:]]
    mine = [v for pair in zip(gu_nears, gu_fars) for v in pair]
    other = [v for pair in zip(gu_nears_other, gu_fars_other) for v in pair]

    down_weight = after(down_weight, sent)
    give = weight_call(give_kernel, "give", depth, part, down_weight)
    got = [flip(v, 1) for v in give]
    dn_near, dn_away = weight_call(join_kernel, "join", 2 * depth, part, down_weight, *got)
    dn_far = flip(after(dn_away, far_x), 2)
    dn_nears = widen([after(dn_near, gu_fars[-1])])

    hidden = up_call([near, far], [near_x, far_x], mine, other)
    hidden = after(hidden, dn_nears[-1])
    dn_far = after(dn_far, hidden)
    dn_fars = widen([dn_far])
    nears = [(v, flip(after(v, hidden), 1)) for v in dn_nears]
    fars = [(dn_far, flip(dn_far, 1))]

    chunks, crossed = [], []
    for m in range(rows):
        parts = 2 if m == rows - 1 else 1
        if m > 0:
            fars.append((dn_fars[m], flip(after(dn_fars[m], sends[0]), 1)))
        sends = down_call(after(hidden, *crossed), nears[m], fars[m], True, parts)
        keeps = down_call(after(hidden, sends[0]), nears[m], fars[m], False, parts)
        crossed = []
        for i, keep in enumerate(keeps):
            crossed.append(flip(sends[parts - 1 - i], 2))
            total = crossed[-1]
            if parts == 1:
                size = total.shape[1] // 2
                total = jnp.concatenate([total[:, size:], total[:, :size]], axis=1)
            total = keep + total.astype(jnp.float32)
            for bit in zone_bits:
                size = total.shape[0] // 2
                moved = total[size:].astype(jnp.bfloat16)
                total = total[:size] + hop(moved, bit).astype(jnp.float32)
            chunks.append(total)
    branch = swap_blocks(jnp.concatenate(chunks, axis=1), me // 2, 2 * rows)
    total = stream_in + branch
    return (total.astype(jnp.bfloat16), normalize(total, final_gain).astype(jnp.bfloat16))


def solution(mesh):
    tokens = P(("dp", "expert"), None)
    weights = P("expert", "dp", None)
    return jax.shard_map(
        body,
        mesh=mesh,
        in_specs=(tokens, tokens, P(), P(), P(), tokens, tokens, P(), weights, weights),
        out_specs=(tokens, tokens),
        check_vma=False,
    )
```

```python
import functools

import jax
import jax.numpy as jnp
from jax import lax
from jax.experimental import pallas as pl
from jax.experimental.pallas import tpu as pltpu
from jax.sharding import PartitionSpec as P

EPS = 1e-06
LOGIT_SCALE = 0.5
LANES = 128
LOW = 64
QUAD = 4


def normalize(values, gain):
    return values * lax.rsqrt(jnp.mean(values * values, axis=-1, keepdims=True) + EPS) * gain


def after(values, *others):
    return lax.optimization_barrier((values, *others))[0]


def after_all(values, *others):
    return list(lax.optimization_barrier((*values, *others)))[: len(values)]


def swap_lanes(values, index, blocks):
    width = values.shape[1]
    size = width // blocks
    lane = lax.broadcasted_iota(jnp.int32, values.shape, 1)
    bit = 1
    while bit < blocks:
        step = bit * size
        upper = (lane // step) % 2 == 1
        swapped = jnp.where(
            upper, pltpu.roll(values, step, 1), pltpu.roll(values, width - step, 1)
        )
        values = jnp.where((index & bit) != 0, swapped, values)
        bit *= 2
    return values


def front_kernel(
    ranks,
    att_ref,
    res_ref,
    w_ref,
    gain_ref,
    routes_ref,
    logits_ref,
    placed_ref,
    stream_ref,
    sent_ref,
    keep_ref,
):
    step = pl.program_id(0)
    cols = w_ref.shape[1]
    width = att_ref.shape[1]
    mixed = res_ref[...].astype(jnp.float32) + jnp.dot(
        att_ref[...], w_ref[...], preferred_element_type=jnp.float32
    )
    stored = mixed.astype(jnp.bfloat16)
    stream_ref[...] = stored
    keep_ref[:, pl.ds(pl.multiple_of(step * cols, cols), cols)] = stored.astype(jnp.float32)

    @pl.when(step == pl.num_programs(0) - 1)
    def _():
        normed = normalize(keep_ref[...], gain_ref[...])
        sent_ref[:, :width] = swap_lanes(normed, lax.axis_index("dp") // 2, ranks // 2).astype(jnp.bfloat16)
        scores = jnp.exp(logits_ref[...].astype(jnp.float32) * LOGIT_SCALE)
        gates = scores / jnp.sum(scores, axis=1, keepdims=True)
        routes = routes_ref[...]
        spread = jnp.zeros((gates.shape[0], LANES), jnp.float32)
        for k in range(gates.shape[1]):
            hit = routes[:, k : k + 1] == placed_ref[...]
            spread = jnp.where(hit, gates[:, k : k + 1], spread)
        high = spread.astype(jnp.bfloat16).astype(jnp.float32)
        lane = lax.broadcasted_iota(jnp.int32, spread.shape, 1)
        sent_ref[:, width:] = jnp.where(lane < LOW, high, spread - high).astype(jnp.bfloat16)


def front_call(ranks, attended, residual, weight, gain, routes, logits, placement):
    tok, width = attended.shape
    steps = 4
    cols = width // steps
    padded = jnp.pad(placement, (0, LOW - placement.shape[0]), constant_values=-1)
    placed = jnp.concatenate([padded, padded])[None, :]
    whole = lambda shape: pl.BlockSpec(shape, lambda i: (0, 0))
    return pl.pallas_call(
        functools.partial(front_kernel, ranks),
        grid=(steps,),
        in_specs=[
            whole((tok, width)),
            pl.BlockSpec((tok, cols), lambda i: (0, i)),
            pl.BlockSpec((width, cols), lambda i: (0, i)),
            whole((1, width)),
            whole(routes.shape),
            whole(logits.shape),
            whole((1, LANES)),
        ],
        out_specs=[
            pl.BlockSpec((tok, cols), lambda i: (0, i)),
            whole((tok, width + LANES)),
        ],
        out_shape=[
            jax.ShapeDtypeStruct((tok, width), jnp.bfloat16),
            jax.ShapeDtypeStruct((tok, width + LANES), jnp.bfloat16),
        ],
        scratch_shapes=[pltpu.VMEM((tok, width), jnp.float32)],
        compiler_params=pltpu.CompilerParams(vmem_limit_bytes=12 * 1024 * 1024),
        cost_estimate=pl.CostEstimate(flops=1, bytes_accessed=1, transcendentals=0),
        name="front",
    )(attended, residual, weight, gain[None, :], routes, logits, placed)


def cut(weight, out_ref, rows, part, c, s):
    for b in range(out_ref.shape[2] // part):
        at = pl.multiple_of(b * QUAD * part + (2 * c + s) * part, part)
        out_ref[:, rows, b * part : (b + 1) * part] = weight[:, :, pl.ds(at, part)]


def give_kernel(part, w_ref, near_ref, away_ref):
    core, side = lax.axis_index("dp") % 2, (lax.axis_index("dp") // 2) % 2
    cut(w_ref, near_ref, slice(None), part, 1 - core, side)
    cut(w_ref, away_ref, slice(None), part, 1 - core, 1 - side)


def join_kernel(part, w_ref, near_in_ref, away_in_ref, near_ref, away_ref):
    core, side = lax.axis_index("dp") % 2, (lax.axis_index("dp") // 2) % 2
    depth = w_ref.shape[1]
    here = pl.ds(pl.multiple_of(core * depth, depth), depth)
    there = pl.ds(pl.multiple_of((1 - core) * depth, depth), depth)
    cut(w_ref, near_ref, here, part, core, side)
    cut(w_ref, away_ref, here, part, core, 1 - side)
    near_ref[:, there, :] = near_in_ref[...]
    away_ref[:, there, :] = away_in_ref[...]


def weight_call(kernel, name, depth, part, weight, *received):
    local, _, cols = weight.shape
    out = jax.ShapeDtypeStruct((local, depth, cols // QUAD), jnp.bfloat16)
    whole = lambda v: pl.BlockSpec(v.shape, lambda i: (0, 0, 0))
    return pl.pallas_call(
        functools.partial(kernel, part),
        grid=(1,),
        in_specs=[whole(v) for v in (weight, *received)],
        out_specs=[whole(out)] * 2,
        out_shape=[out] * 2,
        compiler_params=pltpu.CompilerParams(vmem_limit_bytes=16 * 1024 * 1024),
        cost_estimate=pl.CostEstimate(flops=1, bytes_accessed=1, transcendentals=0),
        name=name,
    )(weight, *received)


def up_kernel(rows, count, *refs):
    here, away = refs[:count], refs[count : 2 * count]
    pieces = refs[2 * count : 2 * count + 4 * rows]
    out_ref, x_ref = refs[2 * count + 4 * rows :]
    zone = lax.axis_index("expert")
    local, half, width = pieces[0].shape
    part = width // 2
    feats = x_ref.shape[1] - LANES
    middle = x_ref.shape[0] // 2

    at = 0
    for block, across in zip(here, away):
        some = slice(at, at + block.shape[0])
        x_ref[some, :] = block[...]
        some = slice(middle + at, middle + at + block.shape[0])
        for j in range(2 * rows):
            to, come = j * half, (j ^ 1) * half
            x_ref[some, to : to + half] = across[:, come : come + half]
        x_ref[some, feats:] = across[:, feats:]
        at += block.shape[0]

    lane = lax.broadcasted_iota(jnp.int32, (LANES, width), 0)
    for e in range(local):
        mine, other = (
            jnp.concatenate([p[e] for p in pieces[2 * i * rows : 2 * (i + 1) * rows]], axis=0)
            for i in range(2)
        )
        w = jnp.concatenate(
            [mine[:, :part], other[:, :part], mine[:, part:], other[:, part:]], axis=1
        )
        slot = zone * local + e
        pick = jnp.where((lane == slot) | (lane == slot + LOW), 0.5, 0.0).astype(jnp.bfloat16)
        acc = jnp.dot(x_ref[:, :feats], w, preferred_element_type=jnp.float32)
        gate = jnp.dot(x_ref[:, feats:], pick, preferred_element_type=jnp.float32)
        g, u = acc[:, :width], acc[:, width:]
        out_ref[:, e * width : (e + 1) * width] = (
            (g + g * jnp.tanh(0.5 * g)) * (u * gate)
        ).astype(jnp.bfloat16)


def up_call(here, away, mine, other):
    local, _, cols = mine[0].shape
    lanes = here[0].shape[1]
    tokens = 2 * sum(v.shape[0] for v in here)
    operands = [*here, *away, *mine, *other]
    return pl.pallas_call(
        functools.partial(up_kernel, len(mine) // 2, len(here)),
        in_specs=[pl.BlockSpec(memory_space=pltpu.VMEM)] * len(operands),
        out_specs=pl.BlockSpec(memory_space=pltpu.VMEM),
        scratch_shapes=[pltpu.VMEM((tokens, lanes), jnp.bfloat16)],
        out_shape=jax.ShapeDtypeStruct((tokens, local * cols), jnp.bfloat16),
        compiler_params=pltpu.CompilerParams(vmem_limit_bytes=28 * 1024 * 1024),
        cost_estimate=pl.CostEstimate(flops=1, bytes_accessed=1, transcendentals=0),
        name="up",
    )(*operands)


def product(hidden, mine, other):
    w = [part[e] for e in range(mine.shape[0]) for part in (mine, other)]
    return lax.dot_general(
        hidden,
        jnp.concatenate(w, axis=1),
        (((1,), (1,)), ((), ())),
        preferred_element_type=jnp.float32,
    )


def down_kernel(start, h_ref, near_ref, near_other_ref, far_ref, far_other_ref, *out_refs):
    rows = out_refs[0].shape[0]
    feats = near_ref.shape[1]
    hidden = h_ref[start : start + rows, :]
    for j, pair in enumerate(((near_ref, near_other_ref), (far_ref, far_other_ref))):
        partial = product(hidden, *pair)
        if len(out_refs) == 2:
            out_refs[j][...] = partial.astype(out_refs[j].dtype)
        else:
            out_refs[0][:, j * feats : (j + 1) * feats] = partial.astype(out_refs[0].dtype)


def down_call(hidden, near, far, send, parts):
    tokens = hidden.shape[0] // 2
    feats = 2 * near[0].shape[1] // parts
    kind = jnp.bfloat16 if send else jnp.float32
    out = [jax.ShapeDtypeStruct((tokens, feats), kind)] * parts
    return pl.pallas_call(
        functools.partial(down_kernel, tokens if send else 0),
        in_specs=[pl.BlockSpec(memory_space=pltpu.VMEM)] * 5,
        out_specs=[pl.BlockSpec(memory_space=pltpu.VMEM)] * parts,
        out_shape=out,
        compiler_params=pltpu.CompilerParams(vmem_limit_bytes=16 * 1024 * 1024),
        cost_estimate=pl.CostEstimate(flops=1, bytes_accessed=1, transcendentals=0),
        name="down",
    )(hidden, *near, *far)


def finish_kernel(blocks, stored_ref, gain_ref, *refs):
    parts, (stream_ref, normed_ref, sum_ref) = refs[:-3], refs[-3:]
    at = 0
    for i in range(len(parts) // 2):
        width = parts[2 * i].shape[1]
        sum_ref[:, at : at + width] = parts[2 * i][...] + parts[2 * i + 1][...].astype(jnp.float32)
        at += width
    branch = swap_lanes(sum_ref[...], lax.axis_index("dp") // 2, blocks)
    total = stored_ref[...].astype(jnp.float32) + branch
    stream_ref[...] = total.astype(jnp.bfloat16)
    normed_ref[...] = normalize(total, gain_ref[...]).astype(jnp.bfloat16)


def finish_call(blocks, stored, gain, chunks):
    vmem = pl.BlockSpec(memory_space=pltpu.VMEM)
    operands = [v for chunk in chunks for v in chunk]
    return pl.pallas_call(
        functools.partial(finish_kernel, blocks),
        in_specs=[vmem] * (2 + len(operands)),
        out_specs=[vmem] * 2,
        out_shape=[jax.ShapeDtypeStruct(stored.shape, jnp.bfloat16)] * 2,
        scratch_shapes=[pltpu.VMEM(stored.shape, jnp.float32)],
        compiler_params=pltpu.CompilerParams(vmem_limit_bytes=12 * 1024 * 1024),
        cost_estimate=pl.CostEstimate(flops=1, bytes_accessed=1, transcendentals=0),
        name="finish",
    )(stored, gain[None, :], *operands)


def body(
    attended,
    residual,
    out_weight,
    norm_gain,
    final_gain,
    routes,
    gate_logits,
    placement,
    gate_up,
    down_weight,
):
    ranks = lax.axis_size("dp")
    zones = lax.axis_size("expert")
    rows = ranks // QUAD
    me = lax.axis_index("dp")
    hid = down_weight.shape[2]
    part = hid // QUAD

    def flip(values, bit):
        return lax.ppermute(values, "dp", [(i, i ^ bit) for i in range(ranks)])

    def hop(values, bit):
        return lax.ppermute(values, "expert", [(i, i ^ bit) for i in range(zones)])

    def widen(pieces):
        bit = 1
        while bit < rows:
            pieces = pieces + [flip(p, bit * QUAD) for p in pieces]
            bit *= 2
        return pieces

    zone_bits = []
    while 1 << len(zone_bits) < zones:
        zone_bits.append(1 << len(zone_bits))
    depth = gate_up.shape[1]
    give = weight_call(give_kernel, "give", depth, part, gate_up)
    got = [flip(v, 1) for v in give]
    gu_near, gu_away = weight_call(join_kernel, "join", 2 * depth, part, gate_up, *got)
    gu_far = flip(gu_away, 2)
    gu_nears = widen([gu_near])

    stored, sent = front_call(
        ranks,
        after(attended, give[0]),
        residual,
        out_weight,
        norm_gain,
        routes,
        gate_logits,
        placement,
    )
    near = sent
    for bit in reversed(zone_bits[1:]):
        near = jnp.concatenate([near, hop(near, bit)], axis=0)
    far = hop(near, 1)
    gu_near_other = flip(gu_near, 1)
    near_x = flip(after(near, gu_near_other), 2)
    gu_fars = widen([after(gu_far, gu_nears[-1])])
    gu_nears_other = [gu_near_other] + [flip(v, 1) for v in gu_nears[1:]]
    gu_far_other = flip(gu_far, 1)
    far_x = flip(after(far, near_x, gu_far_other, *gu_nears_other[1:]), 2)
    gu_fars_other = [gu_far_other] + [flip(v, 1) for v in gu_fars[1:]]
    mine = [v for pair in zip(gu_nears, gu_fars) for v in pair]
    other = [v for pair in zip(gu_nears_other, gu_fars_other) for v in pair]

    down_weight = after(down_weight, sent)
    give = weight_call(give_kernel, "give", depth, part, down_weight)
    got = [flip(v, 1) for v in give]
    dn_near, dn_away = weight_call(join_kernel, "join", 2 * depth, part, down_weight, *got)
    dn_far = flip(after(dn_away, far_x), 2)
    dn_nears = widen([after(dn_near, gu_fars[-1])])

    hidden = up_call([near, far], [near_x, far_x], mine, other)
    hidden = after(hidden, dn_nears[-1])
    dn_far = after(dn_far, hidden)
    dn_fars = widen([dn_far])
    nears = [(v, flip(after(v, hidden), 1)) for v in dn_nears]
    fars = [(dn_far, flip(dn_far, 1))]

    chunks, crossed = [], []
    for m in range(rows):
        parts = 2 if m == rows - 1 else 1
        if m > 0:
            fars.append((dn_fars[m], flip(after(dn_fars[m], sends[0]), 1)))
        sends = down_call(after(hidden, *crossed), nears[m], fars[m], True, parts)
        keeps = down_call(after(hidden, sends[0]), nears[m], fars[m], False, parts)
        crossed = []
        for i, keep in enumerate(keeps):
            crossed.append(flip(sends[parts - 1 - i], 2))
            total = crossed[-1]
            if parts == 1:
                size = total.shape[1] // 2
                total = jnp.concatenate([total[:, size:], total[:, :size]], axis=1)
            total = keep + total.astype(jnp.float32)
            for bit in zone_bits:
                size = total.shape[0] // 2
                moved = total[size:].astype(jnp.bfloat16)
                if bit == zone_bits[-1] and m == rows - 1:
                    moved = after(moved, chunks[0][1])
                received = hop(moved, bit)
                total = total[:size]
                if bit != zone_bits[-1]:
                    total = total + received.astype(jnp.float32)
            chunks.append((total, received))
    return tuple(finish_call(2 * rows, stored, final_gain, chunks))


def solution(mesh):
    tokens = P(("dp", "expert"), None)
    weights = P("expert", "dp", None)
    return jax.shard_map(
        body,
        mesh=mesh,
        in_specs=(tokens, tokens, P(), P(), P(), tokens, tokens, P(), weights, weights),
        out_specs=(tokens, tokens),
        check_vma=False,
    )
```

```python
import functools

import jax
import jax.numpy as jnp
from jax import lax
from jax.experimental import pallas as pl
from jax.experimental.pallas import tpu as pltpu
from jax.sharding import PartitionSpec as P

EPS = 1e-06
LOGIT_SCALE = 0.5
LANES = 128
LOW = 64
QUAD = 4


def normalize(values, gain):
    return values * lax.rsqrt(jnp.mean(values * values, axis=-1, keepdims=True) + EPS) * gain


def after(values, *others):
    return lax.optimization_barrier((values, *others))[0]


def after_all(values, *others):
    return list(lax.optimization_barrier((*values, *others)))[: len(values)]


def swap_lanes(values, index, blocks):
    width = values.shape[1]
    size = width // blocks
    lane = lax.broadcasted_iota(jnp.int32, values.shape, 1)
    bit = 1
    while bit < blocks:
        step = bit * size
        upper = (lane // step) % 2 == 1
        swapped = jnp.where(
            upper, pltpu.roll(values, step, 1), pltpu.roll(values, width - step, 1)
        )
        values = jnp.where((index & bit) != 0, swapped, values)
        bit *= 2
    return values


def front_kernel(
    ranks,
    att_ref,
    res_ref,
    w_ref,
    gain_ref,
    routes_ref,
    logits_ref,
    placed_ref,
    stream_ref,
    sent_ref,
    keep_ref,
):
    step = pl.program_id(0)
    cols = w_ref.shape[1]
    width = att_ref.shape[1]
    mixed = res_ref[...].astype(jnp.float32) + jnp.dot(
        att_ref[...], w_ref[...], preferred_element_type=jnp.float32
    )
    stored = mixed.astype(jnp.bfloat16)
    stream_ref[...] = stored
    keep_ref[:, pl.ds(pl.multiple_of(step * cols, cols), cols)] = stored.astype(jnp.float32)

    @pl.when(step == pl.num_programs(0) - 1)
    def _():
        normed = normalize(keep_ref[...], gain_ref[...])
        sent_ref[:, :width] = swap_lanes(normed, lax.axis_index("dp") // 2, ranks // 2).astype(jnp.bfloat16)
        scores = jnp.exp(logits_ref[...].astype(jnp.float32) * LOGIT_SCALE)
        gates = scores / jnp.sum(scores, axis=1, keepdims=True)
        routes = routes_ref[...]
        spread = jnp.zeros((gates.shape[0], LANES), jnp.float32)
        for k in range(gates.shape[1]):
            hit = routes[:, k : k + 1] == placed_ref[...]
            spread = jnp.where(hit, gates[:, k : k + 1], spread)
        high = spread.astype(jnp.bfloat16).astype(jnp.float32)
        lane = lax.broadcasted_iota(jnp.int32, spread.shape, 1)
        sent_ref[:, width:] = jnp.where(lane < LOW, high, spread - high).astype(jnp.bfloat16)


def front_call(ranks, attended, residual, weight, gain, routes, logits, placement):
    tok, width = attended.shape
    steps = 4
    cols = width // steps
    padded = jnp.pad(placement, (0, LOW - placement.shape[0]), constant_values=-1)
    placed = jnp.concatenate([padded, padded])[None, :]
    whole = lambda shape: pl.BlockSpec(shape, lambda i: (0, 0))
    return pl.pallas_call(
        functools.partial(front_kernel, ranks),
        grid=(steps,),
        in_specs=[
            whole((tok, width)),
            pl.BlockSpec((tok, cols), lambda i: (0, i)),
            pl.BlockSpec((width, cols), lambda i: (0, i)),
            whole((1, width)),
            whole(routes.shape),
            whole(logits.shape),
            whole((1, LANES)),
        ],
        out_specs=[
            pl.BlockSpec((tok, cols), lambda i: (0, i)),
            whole((tok, width + LANES)),
        ],
        out_shape=[
            jax.ShapeDtypeStruct((tok, width), jnp.bfloat16),
            jax.ShapeDtypeStruct((tok, width + LANES), jnp.bfloat16),
        ],
        scratch_shapes=[pltpu.VMEM((tok, width), jnp.float32)],
        compiler_params=pltpu.CompilerParams(vmem_limit_bytes=12 * 1024 * 1024),
        cost_estimate=pl.CostEstimate(flops=1, bytes_accessed=1, transcendentals=0),
        name="front",
    )(attended, residual, weight, gain[None, :], routes, logits, placed)


def cut(weight, out_ref, rows, part, c, s):
    for b in range(out_ref.shape[2] // part):
        at = pl.multiple_of(b * QUAD * part + (2 * c + s) * part, part)
        out_ref[:, rows, b * part : (b + 1) * part] = weight[:, :, pl.ds(at, part)]


def give_kernel(part, w_ref, near_ref, away_ref):
    core, side = lax.axis_index("dp") % 2, (lax.axis_index("dp") // 2) % 2
    cut(w_ref, near_ref, slice(None), part, 1 - core, side)
    cut(w_ref, away_ref, slice(None), part, 1 - core, 1 - side)


def join_kernel(part, w_ref, near_in_ref, away_in_ref, near_ref, away_ref):
    core, side = lax.axis_index("dp") % 2, (lax.axis_index("dp") // 2) % 2
    depth = w_ref.shape[1]
    here = pl.ds(pl.multiple_of(core * depth, depth), depth)
    there = pl.ds(pl.multiple_of((1 - core) * depth, depth), depth)
    cut(w_ref, near_ref, here, part, core, side)
    cut(w_ref, away_ref, here, part, core, 1 - side)
    near_ref[:, there, :] = near_in_ref[...]
    away_ref[:, there, :] = away_in_ref[...]


def weight_call(kernel, name, depth, part, weight, *received):
    local, _, cols = weight.shape
    out = jax.ShapeDtypeStruct((local, depth, cols // QUAD), jnp.bfloat16)
    whole = lambda v: pl.BlockSpec(v.shape, lambda i: (0, 0, 0))
    return pl.pallas_call(
        functools.partial(kernel, part),
        grid=(1,),
        in_specs=[whole(v) for v in (weight, *received)],
        out_specs=[whole(out)] * 2,
        out_shape=[out] * 2,
        compiler_params=pltpu.CompilerParams(vmem_limit_bytes=16 * 1024 * 1024),
        cost_estimate=pl.CostEstimate(flops=1, bytes_accessed=1, transcendentals=0),
        name=name,
    )(weight, *received)


def up_kernel(rows, count, *refs):
    here, away = refs[:count], refs[count : 2 * count]
    pieces = refs[2 * count : 2 * count + 4 * rows]
    out_ref, x_ref = refs[2 * count + 4 * rows :]
    zone = lax.axis_index("expert")
    local, half, width = pieces[0].shape
    part = width // 2
    feats = x_ref.shape[1] - LANES
    middle = x_ref.shape[0] // 2

    at = 0
    for block, across in zip(here, away):
        some = slice(at, at + block.shape[0])
        x_ref[some, :] = block[...]
        some = slice(middle + at, middle + at + block.shape[0])
        for j in range(2 * rows):
            to, come = j * half, (j ^ 1) * half
            x_ref[some, to : to + half] = across[:, come : come + half]
        x_ref[some, feats:] = across[:, feats:]
        at += block.shape[0]

    lane = lax.broadcasted_iota(jnp.int32, (LANES, width), 0)
    for e in range(local):
        mine, other = (
            jnp.concatenate([p[e] for p in pieces[2 * i * rows : 2 * (i + 1) * rows]], axis=0)
            for i in range(2)
        )
        w = jnp.concatenate(
            [mine[:, :part], other[:, :part], mine[:, part:], other[:, part:]], axis=1
        )
        slot = zone * local + e
        pick = jnp.where((lane == slot) | (lane == slot + LOW), 0.5, 0.0).astype(jnp.bfloat16)
        acc = jnp.dot(x_ref[:, :feats], w, preferred_element_type=jnp.float32)
        gate = jnp.dot(x_ref[:, feats:], pick, preferred_element_type=jnp.float32)
        g, u = acc[:, :width], acc[:, width:]
        out_ref[:, e * width : (e + 1) * width] = (
            (g + g * jnp.tanh(0.5 * g)) * (u * gate)
        ).astype(jnp.bfloat16)


def up_call(here, away, mine, other):
    local, _, cols = mine[0].shape
    lanes = here[0].shape[1]
    tokens = 2 * sum(v.shape[0] for v in here)
    operands = [*here, *away, *mine, *other]
    return pl.pallas_call(
        functools.partial(up_kernel, len(mine) // 2, len(here)),
        in_specs=[pl.BlockSpec(memory_space=pltpu.VMEM)] * len(operands),
        out_specs=pl.BlockSpec(memory_space=pltpu.VMEM),
        scratch_shapes=[pltpu.VMEM((tokens, lanes), jnp.bfloat16)],
        out_shape=jax.ShapeDtypeStruct((tokens, local * cols), jnp.bfloat16),
        compiler_params=pltpu.CompilerParams(vmem_limit_bytes=28 * 1024 * 1024),
        cost_estimate=pl.CostEstimate(flops=1, bytes_accessed=1, transcendentals=0),
        name="up",
    )(*operands)


def product(hidden, mine, other):
    w = [part[e] for e in range(mine.shape[0]) for part in (mine, other)]
    return lax.dot_general(
        hidden,
        jnp.concatenate(w, axis=1),
        (((1,), (1,)), ((), ())),
        preferred_element_type=jnp.float32,
    )


def down_kernel(start, h_ref, near_ref, near_other_ref, far_ref, far_other_ref, *out_refs):
    rows = out_refs[0].shape[0]
    feats = near_ref.shape[1]
    hidden = h_ref[start : start + rows, :]
    for j, pair in enumerate(((near_ref, near_other_ref), (far_ref, far_other_ref))):
        partial = product(hidden, *pair)
        if len(out_refs) == 2:
            out_refs[j][...] = partial.astype(out_refs[j].dtype)
        else:
            out_refs[0][:, j * feats : (j + 1) * feats] = partial.astype(out_refs[0].dtype)


def down_call(hidden, near, far, send, parts):
    tokens = hidden.shape[0] // 2
    feats = 2 * near[0].shape[1] // parts
    kind = jnp.bfloat16 if send else jnp.float32
    out = [jax.ShapeDtypeStruct((tokens, feats), kind)] * parts
    return pl.pallas_call(
        functools.partial(down_kernel, tokens if send else 0),
        in_specs=[pl.BlockSpec(memory_space=pltpu.VMEM)] * 5,
        out_specs=[pl.BlockSpec(memory_space=pltpu.VMEM)] * parts,
        out_shape=out,
        compiler_params=pltpu.CompilerParams(vmem_limit_bytes=16 * 1024 * 1024),
        cost_estimate=pl.CostEstimate(flops=1, bytes_accessed=1, transcendentals=0),
        name="down",
    )(hidden, *near, *far)


def finish_kernel(blocks, stored_ref, gain_ref, *refs):
    parts, (stream_ref, normed_ref, sum_ref) = refs[:-3], refs[-3:]
    at = 0
    for i in range(len(parts) // 2):
        width = parts[2 * i].shape[1]
        sum_ref[:, at : at + width] = parts[2 * i][...] + parts[2 * i + 1][...].astype(jnp.float32)
        at += width
    branch = swap_lanes(sum_ref[...], lax.axis_index("dp") // 2, blocks)
    total = stored_ref[...].astype(jnp.float32) + branch
    stream_ref[...] = total.astype(jnp.bfloat16)
    normed_ref[...] = normalize(total, gain_ref[...]).astype(jnp.bfloat16)


def finish_call(blocks, stored, gain, chunks):
    vmem = pl.BlockSpec(memory_space=pltpu.VMEM)
    operands = [v for chunk in chunks for v in chunk]
    return pl.pallas_call(
        functools.partial(finish_kernel, blocks),
        in_specs=[vmem] * (2 + len(operands)),
        out_specs=[vmem] * 2,
        out_shape=[jax.ShapeDtypeStruct(stored.shape, jnp.bfloat16)] * 2,
        scratch_shapes=[pltpu.VMEM(stored.shape, jnp.float32)],
        compiler_params=pltpu.CompilerParams(vmem_limit_bytes=12 * 1024 * 1024),
        cost_estimate=pl.CostEstimate(flops=1, bytes_accessed=1, transcendentals=0),
        name="finish",
    )(stored, gain[None, :], *operands)


def body(
    attended,
    residual,
    out_weight,
    norm_gain,
    final_gain,
    routes,
    gate_logits,
    placement,
    gate_up,
    down_weight,
):
    ranks = lax.axis_size("dp")
    zones = lax.axis_size("expert")
    rows = ranks // QUAD
    me = lax.axis_index("dp")
    hid = down_weight.shape[2]
    part = hid // QUAD

    def flip(values, bit):
        return lax.ppermute(values, "dp", [(i, i ^ bit) for i in range(ranks)])

    def hop(values, bit):
        return lax.ppermute(values, "expert", [(i, i ^ bit) for i in range(zones)])

    def widen(pieces):
        bit = 1
        while bit < rows:
            pieces = pieces + [flip(p, bit * QUAD) for p in pieces]
            bit *= 2
        return pieces

    zone_bits = []
    while 1 << len(zone_bits) < zones:
        zone_bits.append(1 << len(zone_bits))
    depth = gate_up.shape[1]
    give = weight_call(give_kernel, "give", depth, part, gate_up)
    got = [flip(v, 1) for v in give]
    gu_near, gu_away = weight_call(join_kernel, "join", 2 * depth, part, gate_up, *got)
    gu_far = flip(gu_away, 2)
    gu_nears = widen([gu_near])

    stored, sent = front_call(
        ranks,
        after(attended, give[0]),
        residual,
        out_weight,
        norm_gain,
        routes,
        gate_logits,
        placement,
    )
    near = sent
    for bit in reversed(zone_bits[1:]):
        near = jnp.concatenate([near, hop(near, bit)], axis=0)
    far = hop(near, 1)
    gu_near_other = flip(gu_near, 1)
    near_x = flip(after(near, gu_near_other), 2)
    gu_fars = widen([after(gu_far, gu_nears[-1])])
    gu_nears_other = [gu_near_other] + [flip(v, 1) for v in gu_nears[1:]]
    gu_far_other = flip(gu_far, 1)
    far_x = flip(after(far, near_x), 2)
    gu_fars_other = [gu_far_other] + [flip(v, 1) for v in gu_fars[1:]]
    mine = [v for pair in zip(gu_nears, gu_fars) for v in pair]
    other = [v for pair in zip(gu_nears_other, gu_fars_other) for v in pair]

    down_weight = after(down_weight, sent)
    give = weight_call(give_kernel, "give", depth, part, down_weight)
    got = [flip(v, 1) for v in give]
    dn_near, dn_away = weight_call(join_kernel, "join", 2 * depth, part, down_weight, *got)
    dn_far = flip(after(dn_away, far_x), 2)
    dn_nears = widen([after(dn_near, gu_fars[-1])])

    hidden = up_call([near, far], [near_x, far_x], mine, other)
    hidden = after(hidden, dn_nears[-1])
    dn_far = after(dn_far, hidden)
    dn_fars = widen([dn_far])
    nears = [(v, flip(after(v, hidden), 1)) for v in dn_nears]
    fars = [(dn_far, flip(dn_far, 1))]

    chunks, crossed = [], []
    for m in range(rows):
        parts = 2 if m == rows - 1 else 1
        if m > 0:
            fars.append((dn_fars[m], flip(after(dn_fars[m], sends[0]), 1)))
        sends = down_call(after(hidden, *crossed), nears[m], fars[m], True, parts)
        keeps = down_call(after(hidden, sends[0]), nears[m], fars[m], False, parts)
        crossed = []
        for i, keep in enumerate(keeps):
            crossed.append(flip(sends[parts - 1 - i], 2))
            total = crossed[-1]
            if parts == 1:
                size = total.shape[1] // 2
                total = jnp.concatenate([total[:, size:], total[:, :size]], axis=1)
            total = keep + total.astype(jnp.float32)
            for bit in zone_bits:
                size = total.shape[0] // 2
                moved = total[size:].astype(jnp.bfloat16)
                if bit == zone_bits[-1] and m == rows - 1 and i == 1:
                    moved = after(moved, chunks[0][1])
                received = hop(moved, bit)
                total = total[:size]
                if bit != zone_bits[-1]:
                    total = total + received.astype(jnp.float32)
            chunks.append((total, received))
    return tuple(finish_call(2 * rows, stored, final_gain, chunks))


def solution(mesh):
    tokens = P(("dp", "expert"), None)
    weights = P("expert", "dp", None)
    return jax.shard_map(
        body,
        mesh=mesh,
        in_specs=(tokens, tokens, P(), P(), P(), tokens, tokens, P(), weights, weights),
        out_specs=(tokens, tokens),
        check_vma=False,
    )
```

```python
import functools

import jax
import jax.numpy as jnp
from jax import lax
from jax.experimental import pallas as pl
from jax.experimental.pallas import tpu as pltpu
from jax.sharding import PartitionSpec as P

EPS = 1e-06
LOGIT_SCALE = 0.5
LANES = 128
LOW = 64
QUAD = 4


def normalize(values, gain):
    return values * lax.rsqrt(jnp.mean(values * values, axis=-1, keepdims=True) + EPS) * gain


def after(values, *others):
    return lax.optimization_barrier((values, *others))[0]


def after_all(values, *others):
    return list(lax.optimization_barrier((*values, *others)))[: len(values)]


def swap_lanes(values, index, blocks):
    width = values.shape[1]
    size = width // blocks
    lane = lax.broadcasted_iota(jnp.int32, values.shape, 1)
    bit = 1
    while bit < blocks:
        step = bit * size
        upper = (lane // step) % 2 == 1
        swapped = jnp.where(
            upper, pltpu.roll(values, step, 1), pltpu.roll(values, width - step, 1)
        )
        values = jnp.where((index & bit) != 0, swapped, values)
        bit *= 2
    return values


def front_kernel(
    ranks,
    att_ref,
    res_ref,
    w_ref,
    gain_ref,
    routes_ref,
    logits_ref,
    placed_ref,
    stream_ref,
    sent_ref,
    keep_ref,
):
    step = pl.program_id(0)
    cols = w_ref.shape[1]
    width = att_ref.shape[1]
    mixed = res_ref[...].astype(jnp.float32) + jnp.dot(
        att_ref[...], w_ref[...], preferred_element_type=jnp.float32
    )
    stored = mixed.astype(jnp.bfloat16)
    stream_ref[...] = stored
    keep_ref[:, pl.ds(pl.multiple_of(step * cols, cols), cols)] = stored.astype(jnp.float32)

    @pl.when(step == pl.num_programs(0) - 1)
    def _():
        normed = normalize(keep_ref[...], gain_ref[...])
        sent_ref[:, :width] = swap_lanes(normed, lax.axis_index("dp") // 2, ranks // 2).astype(jnp.bfloat16)
        scores = jnp.exp(logits_ref[...].astype(jnp.float32) * LOGIT_SCALE)
        gates = scores / jnp.sum(scores, axis=1, keepdims=True)
        routes = routes_ref[...]
        spread = jnp.zeros((gates.shape[0], LANES), jnp.float32)
        for k in range(gates.shape[1]):
            hit = routes[:, k : k + 1] == placed_ref[...]
            spread = jnp.where(hit, gates[:, k : k + 1], spread)
        high = spread.astype(jnp.bfloat16).astype(jnp.float32)
        lane = lax.broadcasted_iota(jnp.int32, spread.shape, 1)
        sent_ref[:, width:] = jnp.where(lane < LOW, high, spread - high).astype(jnp.bfloat16)


def front_call(ranks, attended, residual, weight, gain, routes, logits, placement):
    tok, width = attended.shape
    steps = 4
    cols = width // steps
    padded = jnp.pad(placement, (0, LOW - placement.shape[0]), constant_values=-1)
    placed = jnp.concatenate([padded, padded])[None, :]
    whole = lambda shape: pl.BlockSpec(shape, lambda i: (0, 0))
    return pl.pallas_call(
        functools.partial(front_kernel, ranks),
        grid=(steps,),
        in_specs=[
            whole((tok, width)),
            pl.BlockSpec((tok, cols), lambda i: (0, i)),
            pl.BlockSpec((width, cols), lambda i: (0, i)),
            whole((1, width)),
            whole(routes.shape),
            whole(logits.shape),
            whole((1, LANES)),
        ],
        out_specs=[
            pl.BlockSpec((tok, cols), lambda i: (0, i)),
            whole((tok, width + LANES)),
        ],
        out_shape=[
            jax.ShapeDtypeStruct((tok, width), jnp.bfloat16),
            jax.ShapeDtypeStruct((tok, width + LANES), jnp.bfloat16),
        ],
        scratch_shapes=[pltpu.VMEM((tok, width), jnp.float32)],
        compiler_params=pltpu.CompilerParams(vmem_limit_bytes=12 * 1024 * 1024),
        cost_estimate=pl.CostEstimate(flops=1, bytes_accessed=1, transcendentals=0),
        name="front",
    )(attended, residual, weight, gain[None, :], routes, logits, placed)


def cut(weight, out_ref, rows, part, c, s):
    for b in range(out_ref.shape[2] // part):
        at = pl.multiple_of(b * QUAD * part + (2 * c + s) * part, part)
        out_ref[:, rows, b * part : (b + 1) * part] = weight[:, :, pl.ds(at, part)]


def give_kernel(part, w_ref, near_ref, away_ref):
    core, side = lax.axis_index("dp") % 2, (lax.axis_index("dp") // 2) % 2
    cut(w_ref, near_ref, slice(None), part, 1 - core, side)
    cut(w_ref, away_ref, slice(None), part, 1 - core, 1 - side)


def join_kernel(part, w_ref, near_in_ref, away_in_ref, near_ref, away_ref):
    core, side = lax.axis_index("dp") % 2, (lax.axis_index("dp") // 2) % 2
    depth = w_ref.shape[1]
    here = pl.ds(pl.multiple_of(core * depth, depth), depth)
    there = pl.ds(pl.multiple_of((1 - core) * depth, depth), depth)
    cut(w_ref, near_ref, here, part, core, side)
    cut(w_ref, away_ref, here, part, core, 1 - side)
    near_ref[:, there, :] = near_in_ref[...]
    away_ref[:, there, :] = away_in_ref[...]


def weight_call(kernel, name, depth, part, weight, *received):
    local, _, cols = weight.shape
    out = jax.ShapeDtypeStruct((local, depth, cols // QUAD), jnp.bfloat16)
    whole = lambda v: pl.BlockSpec(v.shape, lambda i: (0, 0, 0))
    return pl.pallas_call(
        functools.partial(kernel, part),
        grid=(1,),
        in_specs=[whole(v) for v in (weight, *received)],
        out_specs=[whole(out)] * 2,
        out_shape=[out] * 2,
        compiler_params=pltpu.CompilerParams(vmem_limit_bytes=16 * 1024 * 1024),
        cost_estimate=pl.CostEstimate(flops=1, bytes_accessed=1, transcendentals=0),
        name=name,
    )(weight, *received)


def up_kernel(rows, count, *refs):
    here, away = refs[:count], refs[count : 2 * count]
    pieces = refs[2 * count : 2 * count + 4 * rows]
    out_ref, x_ref = refs[2 * count + 4 * rows :]
    zone = lax.axis_index("expert")
    local, half, width = pieces[0].shape
    part = width // 2
    feats = x_ref.shape[1] - LANES
    middle = x_ref.shape[0] // 2

    at = 0
    for block, across in zip(here, away):
        some = slice(at, at + block.shape[0])
        x_ref[some, :] = block[...]
        some = slice(middle + at, middle + at + block.shape[0])
        for j in range(2 * rows):
            to, come = j * half, (j ^ 1) * half
            x_ref[some, to : to + half] = across[:, come : come + half]
        x_ref[some, feats:] = across[:, feats:]
        at += block.shape[0]

    lane = lax.broadcasted_iota(jnp.int32, (LANES, width), 0)
    for e in range(local):
        mine, other = (
            jnp.concatenate([p[e] for p in pieces[2 * i * rows : 2 * (i + 1) * rows]], axis=0)
            for i in range(2)
        )
        w = jnp.concatenate(
            [mine[:, :part], other[:, :part], mine[:, part:], other[:, part:]], axis=1
        )
        slot = zone * local + e
        pick = jnp.where((lane == slot) | (lane == slot + LOW), 0.5, 0.0).astype(jnp.bfloat16)
        acc = jnp.dot(x_ref[:, :feats], w, preferred_element_type=jnp.float32)
        gate = jnp.dot(x_ref[:, feats:], pick, preferred_element_type=jnp.float32)
        g, u = acc[:, :width], acc[:, width:]
        out_ref[:, e * width : (e + 1) * width] = (
            (g + g * jnp.tanh(0.5 * g)) * (u * gate)
        ).astype(jnp.bfloat16)


def up_call(here, away, mine, other):
    local, _, cols = mine[0].shape
    lanes = here[0].shape[1]
    tokens = 2 * sum(v.shape[0] for v in here)
    operands = [*here, *away, *mine, *other]
    return pl.pallas_call(
        functools.partial(up_kernel, len(mine) // 2, len(here)),
        in_specs=[pl.BlockSpec(memory_space=pltpu.VMEM)] * len(operands),
        out_specs=pl.BlockSpec(memory_space=pltpu.VMEM),
        scratch_shapes=[pltpu.VMEM((tokens, lanes), jnp.bfloat16)],
        out_shape=jax.ShapeDtypeStruct((tokens, local * cols), jnp.bfloat16),
        compiler_params=pltpu.CompilerParams(vmem_limit_bytes=28 * 1024 * 1024),
        cost_estimate=pl.CostEstimate(flops=1, bytes_accessed=1, transcendentals=0),
        name="up",
    )(*operands)


def product(hidden, mine, other):
    w = [part[e] for e in range(mine.shape[0]) for part in (mine, other)]
    return lax.dot_general(
        hidden,
        jnp.concatenate(w, axis=1),
        (((1,), (1,)), ((), ())),
        preferred_element_type=jnp.float32,
    )


def down_kernel(start, h_ref, near_ref, near_other_ref, far_ref, far_other_ref, *out_refs):
    rows = out_refs[0].shape[0]
    feats = near_ref.shape[1]
    hidden = h_ref[start : start + rows, :]
    for j, pair in enumerate(((near_ref, near_other_ref), (far_ref, far_other_ref))):
        partial = product(hidden, *pair)
        if len(out_refs) == 2:
            out_refs[j][...] = partial.astype(out_refs[j].dtype)
        else:
            out_refs[0][:, j * feats : (j + 1) * feats] = partial.astype(out_refs[0].dtype)


def down_call(hidden, near, far, send, parts):
    tokens = hidden.shape[0] // 2
    feats = 2 * near[0].shape[1] // parts
    kind = jnp.bfloat16 if send else jnp.float32
    out = [jax.ShapeDtypeStruct((tokens, feats), kind)] * parts
    return pl.pallas_call(
        functools.partial(down_kernel, tokens if send else 0),
        in_specs=[pl.BlockSpec(memory_space=pltpu.VMEM)] * 5,
        out_specs=[pl.BlockSpec(memory_space=pltpu.VMEM)] * parts,
        out_shape=out,
        compiler_params=pltpu.CompilerParams(vmem_limit_bytes=16 * 1024 * 1024),
        cost_estimate=pl.CostEstimate(flops=1, bytes_accessed=1, transcendentals=0),
        name="down",
    )(hidden, *near, *far)


def finish_kernel(blocks, stored_ref, gain_ref, *refs):
    parts, (stream_ref, normed_ref, sum_ref) = refs[:-3], refs[-3:]
    at = 0
    for i in range(len(parts) // 2):
        width = parts[2 * i].shape[1]
        sum_ref[:, at : at + width] = parts[2 * i][...] + parts[2 * i + 1][...].astype(jnp.float32)
        at += width
    branch = swap_lanes(sum_ref[...], lax.axis_index("dp") // 2, blocks)
    total = stored_ref[...].astype(jnp.float32) + branch
    stream_ref[...] = total.astype(jnp.bfloat16)
    normed_ref[...] = normalize(total, gain_ref[...]).astype(jnp.bfloat16)


def finish_call(blocks, stored, gain, chunks):
    vmem = pl.BlockSpec(memory_space=pltpu.VMEM)
    operands = [v for chunk in chunks for v in chunk]
    return pl.pallas_call(
        functools.partial(finish_kernel, blocks),
        in_specs=[vmem] * (2 + len(operands)),
        out_specs=[vmem] * 2,
        out_shape=[jax.ShapeDtypeStruct(stored.shape, jnp.bfloat16)] * 2,
        scratch_shapes=[pltpu.VMEM(stored.shape, jnp.float32)],
        compiler_params=pltpu.CompilerParams(vmem_limit_bytes=12 * 1024 * 1024),
        cost_estimate=pl.CostEstimate(flops=1, bytes_accessed=1, transcendentals=0),
        name="finish",
    )(stored, gain[None, :], *operands)


def body(
    attended,
    residual,
    out_weight,
    norm_gain,
    final_gain,
    routes,
    gate_logits,
    placement,
    gate_up,
    down_weight,
):
    ranks = lax.axis_size("dp")
    zones = lax.axis_size("expert")
    rows = ranks // QUAD
    me = lax.axis_index("dp")
    hid = down_weight.shape[2]
    part = hid // QUAD

    def flip(values, bit):
        return lax.ppermute(values, "dp", [(i, i ^ bit) for i in range(ranks)])

    def hop(values, bit):
        return lax.ppermute(values, "expert", [(i, i ^ bit) for i in range(zones)])

    def widen(pieces):
        bit = 1
        while bit < rows:
            pieces = pieces + [flip(p, bit * QUAD) for p in pieces]
            bit *= 2
        return pieces

    zone_bits = []
    while 1 << len(zone_bits) < zones:
        zone_bits.append(1 << len(zone_bits))
    depth = gate_up.shape[1]
    give = weight_call(give_kernel, "give", depth, part, gate_up)
    got = [flip(v, 1) for v in give]
    gu_near, gu_away = weight_call(join_kernel, "join", 2 * depth, part, gate_up, *got)
    gu_far = flip(gu_away, 2)
    gu_nears = widen([gu_near])

    stored, sent = front_call(
        ranks,
        after(attended, give[0]),
        residual,
        out_weight,
        norm_gain,
        routes,
        gate_logits,
        placement,
    )
    near = sent
    for bit in reversed(zone_bits[1:]):
        near = jnp.concatenate([near, hop(near, bit)], axis=0)
    far = hop(near, 1)
    gu_near_other = flip(gu_near, 1)
    near_x = flip(after(near, gu_near_other), 2)
    gu_fars = widen([after(gu_far, gu_nears[-1])])
    gu_nears_other = [gu_near_other] + [flip(v, 1) for v in gu_nears[1:]]
    gu_far_other = flip(gu_far, 1)
    far_x = flip(after(far, near_x), 2)
    gu_fars_other = [gu_far_other] + [flip(v, 1) for v in gu_fars[1:]]
    mine = [v for pair in zip(gu_nears, gu_fars) for v in pair]
    other = [v for pair in zip(gu_nears_other, gu_fars_other) for v in pair]

    down_weight = after(down_weight, sent)
    give = weight_call(give_kernel, "give", depth, part, down_weight)
    got = [flip(v, 1) for v in give]
    dn_near, dn_away = weight_call(join_kernel, "join", 2 * depth, part, down_weight, *got)
    dn_far = flip(after(dn_away, far_x), 2)
    dn_nears = widen([after(dn_near, gu_fars[-1])])

    hidden = up_call([near, far], [near_x, far_x], mine, other)
    near_first = flip(after(dn_near, hidden), 1)
    hidden = after(hidden, dn_nears[-1])
    dn_far = after(dn_far, hidden)
    dn_fars = widen([dn_far])
    nears = [(dn_near, near_first)] + [(v, flip(after(v, hidden), 1)) for v in dn_nears[1:]]
    fars = [(dn_far, flip(dn_far, 1))]

    chunks, crossed = [], []
    for m in range(rows):
        parts = 2 if m == rows - 1 else 1
        if m > 0:
            fars.append((dn_fars[m], flip(after(dn_fars[m], sends[0]), 1)))
        sends = down_call(after(hidden, *crossed), nears[m], fars[m], True, parts)
        keeps = down_call(after(hidden, sends[0]), nears[m], fars[m], False, parts)
        crossed = []
        for i, keep in enumerate(keeps):
            crossed.append(flip(sends[parts - 1 - i], 2))
            total = crossed[-1]
            if parts == 1:
                size = total.shape[1] // 2
                total = jnp.concatenate([total[:, size:], total[:, :size]], axis=1)
            total = keep + total.astype(jnp.float32)
            for bit in zone_bits:
                size = total.shape[0] // 2
                moved = total[size:].astype(jnp.bfloat16)
                if bit == zone_bits[-1] and m == rows - 1 and i == 1:
                    moved = after(moved, chunks[0][1])
                received = hop(moved, bit)
                total = total[:size]
                if bit != zone_bits[-1]:
                    total = total + received.astype(jnp.float32)
            chunks.append((total, received))
    return tuple(finish_call(2 * rows, stored, final_gain, chunks))


def solution(mesh):
    tokens = P(("dp", "expert"), None)
    weights = P("expert", "dp", None)
    return jax.shard_map(
        body,
        mesh=mesh,
        in_specs=(tokens, tokens, P(), P(), P(), tokens, tokens, P(), weights, weights),
        out_specs=(tokens, tokens),
        check_vma=False,
    )
```
